128 devices in a mesh: car: 8 (over z_hi, x), dom: 16 (over y, z_lo, core).
Axes of the slice: x: 4, y: 4, z: 4 (z_hi: 2, z_lo: 2; z = z_hi * 2 + z_lo), core: 2. Of those that a mesh axis runs over, the one named last changes fastest.
Arguments:
- points: bfloat16 [131072, 768], P(('car', 'dom')), parts along dimension 0, may hold values from -6 to 6
- norm_gain: float32 [768], replicated, may hold values from 0.25 to 1.75
- w_qkv: bfloat16 [768, 2304], replicated, may hold values from -0.12629537 to 0.12629537
- w_out: bfloat16 [768, 768], replicated, may hold values from -0.75 to 0.75
- w_cross_q: bfloat16 [768, 768], replicated, may hold values from -0.12629537 to 0.12629537
- w_cross_kv: bfloat16 [768, 1536], replicated, may hold values from -0.12629537 to 0.12629537
- w_cross_out: bfloat16 [768, 768], replicated, may hold values from -0.75 to 0.75
- live_blocks: int32 [128], P(('car', 'dom')), parts along dimension 0, may hold values from 4 to 8, as said below
- send_blocks: int32 [512], P(('car', 'dom')), parts along dimension 0, may hold values from 0 to 7, as said below
- neighbours: int32 [1024, 8], P(('car', 'dom')), parts along dimension 0, may hold values from 0 to 11, as said below
- neighbour_count: int32 [1024], P(('car', 'dom')), parts along dimension 0, may hold values from 2 to 8
- anchor_index: int32 [32768], P(('car', 'dom')), parts along dimension 0, may hold values from 0 to 1023, as said below
Outputs:
- mixed: bfloat16 [131072, 768], P(('car', 'dom')), parts along dimension 0
The draws below stay inside these ranges and needn't reach their ends.
There are 8 independent parts, one for each index of `car`. The reference program is written for one: setup_inputs(seed, part) draws one part's arguments, and reference() takes and returns one part's arrays. A program takes and returns all parts, laid end to end along the dimension named above; an argument that names none is the same for every part. Nothing has to cross between parts.
Inputs may be any that keep to these rules, and one draw needn't show every extreme that they name: `live_blocks`: some partition of every car has all 8 blocks live. `send_blocks`: the 2 blocks of each list are distinct live blocks of the sending partition. `neighbours`: slot 0 of every block is the block itself; the first partition of a car names no block of a previous one and the last none of a next one; counted slots of a live block name live blocks. `anchor_index`: anchors lie in live blocks of their partition.
All inputs are finite; a program needn't handle non-finite values.
Results may differ from the reference program's by a relative error of at most 0.0086.
Values may be sent and summed in bfloat16 or wider, within the bound.
No kernel may reach another device: no remote copies, remote signals or barrier semaphores. Data moves between devices by JAX's collectives and lax.ppermute only.
A program may use at most 256 MiB of HBM per device.

```python
import jax
import jax.numpy as jnp
from jax import lax

D = 768
HEADS = 12
BLK = 128
NBR = 8
HB = 2
NB_DEV = 8
A_DEV = 256
HEAD_DIM = 64
P_DEV = 1024
POINTS = 16384
ANCHORS = 4096
N_DOM = 16


def live_counts(key):
    base = jax.random.fold_in(key, 101)
    counts = jax.random.randint(base, (N_DOM,), NB_DEV // 2, NB_DEV + 1)
    filled = jax.random.randint(jax.random.fold_in(base, 1), (), 0, N_DOM)
    counts = jnp.where(jnp.arange(N_DOM) == filled, NB_DEV, counts)
    return (counts.astype(jnp.int32), filled)


def draw_points(key, part):
    own_key = jax.random.fold_in(key, 11)
    key_base = jax.random.fold_in(own_key, 0)
    values = jax.random.normal(key_base, (POINTS, D), jnp.float32)
    return jnp.clip(values, -6.0, 6.0).astype(jnp.bfloat16)


def draw_w_qkv(key, part):
    own_key = jax.random.fold_in(key, 21)
    values = jax.random.truncated_normal(own_key, -3.5, 3.5, (D, 3 * D), jnp.float32) * D ** (-0.5)
    return values.astype(jnp.bfloat16)


def draw_w_cross_q(key, part):
    own_key = jax.random.fold_in(key, 22)
    values = jax.random.truncated_normal(own_key, -3.5, 3.5, (D, D), jnp.float32) * D ** (-0.5)
    return values.astype(jnp.bfloat16)


def draw_w_cross_kv(key, part):
    own_key = jax.random.fold_in(key, 23)
    values = jax.random.truncated_normal(own_key, -3.5, 3.5, (D, 2 * D), jnp.float32) * D ** (-0.5)
    return values.astype(jnp.bfloat16)


def draw_live_blocks(key, part):
    counts, filled = live_counts(key)
    return counts


def draw_send_blocks(key, part):
    counts, filled = live_counts(key)
    key = jax.random.fold_in(key, 2)
    order = jnp.arange(NB_DEV)
    scores = jax.random.randint(key, (N_DOM, NB_DEV), 0, 1 << 20) * NB_DEV + order[None, :]
    scores = jnp.where(order[None, :] < counts[:, None], scores, (1 << 30) + order[None, :])
    picked = jnp.argsort(scores, axis=1)[:, :2 * HB]
    return picked.reshape(-1).astype(jnp.int32)


def draw_neighbours(key, part):
    counts, filled = live_counts(key)
    key = jax.random.fold_in(key, 3)
    key_own, key_side, key_which = jax.random.split(key, 3)
    block_total = N_DOM * NB_DEV
    device = jnp.arange(block_total) // NB_DEV
    local = jnp.arange(block_total) % NB_DEV
    live = counts[device]
    own_pick = jax.random.randint(key_own, (block_total, NBR), 0, live[:, None])
    side = jax.random.randint(key_side, (block_total, NBR), 0, 4)
    which = jax.random.randint(key_which, (block_total, NBR), 0, HB)
    from_prev = NB_DEV + which
    from_next = NB_DEV + HB + which
    picked = jnp.where((side == 2) & (device[:, None] > 0), from_prev, jnp.where((side == 3) & (device[:, None] < N_DOM - 1), from_next, own_pick))
    picked = picked.at[:, 0].set(local)
    return picked.astype(jnp.int32)


def draw_neighbour_count(key, part):
    key = jax.random.fold_in(key, 4)
    counts = jax.random.randint(key, (N_DOM * NB_DEV,), 2, NBR + 1)
    return counts.at[0].set(NBR).astype(jnp.int32)


def draw_anchor_index(key, part):
    counts, filled = live_counts(key)
    key = jax.random.fold_in(key, 5)
    picked = jax.random.randint(key, (N_DOM, A_DEV), 0, (counts * BLK)[:, None])
    picked = picked.at[:, 0].set(0)
    picked = picked.at[:, 1].set(1)
    picked = picked.at[filled, 1].set(NB_DEV * BLK - 1)
    return picked.reshape(-1).astype(jnp.int32)


def scatter_about(key, dims, deviation, reach, held_as=jnp.bfloat16):
    values = deviation * jax.random.normal(key, dims, jnp.float32)
    return jnp.clip(values, min=-reach, max=reach).astype(held_as)


def setup_inputs(seed: int = 0, part: int = 0) -> dict:
    keys = jax.random.split(jax.random.key(seed), 13)
    own_keys = jax.random.split(jax.random.fold_in(keys[12], part), 13)
    points = draw_points(jax.random.fold_in(jax.random.fold_in(keys[12], part), 71), part)
    norm_gain = jnp.clip(1.0 + 0.15 * jax.random.normal(keys[1], (D,), jnp.float32), 0.25, 1.75)
    w_qkv = draw_w_qkv(jax.random.fold_in(keys[12], 71), part)
    w_out = scatter_about(keys[3], (D, D), HEAD_DIM ** -0.5, 0.75)
    w_cross_q = draw_w_cross_q(jax.random.fold_in(keys[12], 71), part)
    w_cross_kv = draw_w_cross_kv(jax.random.fold_in(keys[12], 71), part)
    w_cross_out = scatter_about(keys[6], (D, D), HEAD_DIM ** -0.5, 0.75)
    live_blocks = draw_live_blocks(jax.random.fold_in(jax.random.fold_in(keys[12], part), 71), part)
    send_blocks = draw_send_blocks(jax.random.fold_in(jax.random.fold_in(keys[12], part), 71), part)
    neighbours = draw_neighbours(jax.random.fold_in(jax.random.fold_in(keys[12], part), 71), part)
    neighbour_count = draw_neighbour_count(jax.random.fold_in(jax.random.fold_in(keys[12], part), 71), part)
    anchor_index = draw_anchor_index(jax.random.fold_in(jax.random.fold_in(keys[12], part), 71), part)
    return dict(points=points, norm_gain=norm_gain, w_qkv=w_qkv, w_out=w_out, w_cross_q=w_cross_q, w_cross_kv=w_cross_kv, w_cross_out=w_cross_out, live_blocks=live_blocks, send_blocks=send_blocks, neighbours=neighbours, neighbour_count=neighbour_count, anchor_index=anchor_index)


def normalize(points, norm_gain):
    floats = points.astype(jnp.float32)
    factor = lax.rsqrt(lax.optimization_barrier(jnp.mean(floats * floats, axis=-1, keepdims=True)) + 1e-06)
    return (floats * factor * norm_gain).astype(jnp.bfloat16)

def attend(queries, key_rows, value_rows, key_valid):
    row_count = queries.shape[0]
    key_count = key_rows.shape[0]
    head_dim = queries.shape[1] // HEADS
    query_heads = queries.astype(jnp.float32).reshape(row_count, HEADS, head_dim)
    key_heads = key_rows.astype(jnp.float32).reshape(key_count, HEADS, head_dim)
    value_heads = value_rows.astype(jnp.float32).reshape(key_count, HEADS, head_dim)
    scores = jnp.einsum('rhd,khd->hrk', query_heads, key_heads) * head_dim ** (-0.5)
    scores = jnp.where(key_valid[None, None, :], scores, -1e+30)
    row_max = lax.optimization_barrier(jnp.max(scores, axis=-1, keepdims=True))
    expo = jnp.exp(scores - row_max)
    weights = lax.optimization_barrier((expo / lax.optimization_barrier(jnp.sum(expo, axis=-1, keepdims=True))).astype(jnp.bfloat16))
    result = jnp.einsum('hrk,khd->rhd', weights.astype(jnp.float32), value_heads)
    return result.reshape(row_count, HEADS * head_dim).astype(jnp.bfloat16)

def resolve(neighbours, send_blocks):
    block_total = neighbours.shape[0]
    device = jnp.arange(block_total) // NB_DEV
    before = jnp.clip(device - 1, 0, N_DOM - 1)[:, None]
    after = jnp.clip(device + 1, 0, N_DOM - 1)[:, None]
    own_ids = device[:, None] * NB_DEV + neighbours
    prev_slot = jnp.clip(neighbours - NB_DEV, 0, HB - 1)
    from_prev = before * NB_DEV + send_blocks[before * 2 * HB + HB + prev_slot]
    next_slot = jnp.clip(neighbours - NB_DEV - HB, 0, HB - 1)
    from_next = after * NB_DEV + send_blocks[after * 2 * HB + next_slot]
    return jnp.where(neighbours < NB_DEV, own_ids, jnp.where(neighbours < NB_DEV + HB, from_prev, from_next))

def reference(points, norm_gain, w_qkv, w_out, w_cross_q, w_cross_kv, w_cross_out, live_blocks, send_blocks, neighbours, neighbour_count, anchor_index):
    model_width = points.shape[1]
    normed = normalize(points, norm_gain)
    qkv = jnp.dot(normed, w_qkv, preferred_element_type=jnp.float32).astype(jnp.bfloat16)
    block_total = neighbours.shape[0]
    query_blocks = qkv[:, :model_width].reshape(block_total, BLK, model_width)
    key_blocks = qkv[:, model_width:2 * model_width].reshape(block_total, BLK, model_width)
    value_blocks = qkv[:, 2 * model_width:].reshape(block_total, BLK, model_width)
    global_ids = resolve(neighbours, send_blocks)
    slot_valid = jnp.arange(NBR)[None, :] < neighbour_count[:, None]

    def one_block(inputs):
        block_query, block_ids, block_valid = inputs
        key_rows = key_blocks[block_ids].reshape(-1, model_width)
        value_rows = value_blocks[block_ids].reshape(-1, model_width)
        return attend(block_query, key_rows, value_rows, jnp.repeat(block_valid, BLK))
    block_attn = lax.map(one_block, (query_blocks, global_ids, slot_valid)).reshape(-1, model_width)
    block_term = jnp.dot(block_attn, w_out, preferred_element_type=jnp.float32)
    owner = jnp.arange(ANCHORS) // A_DEV
    anchor_rows = normed[owner * P_DEV + anchor_index]
    anchor_kv = jnp.dot(anchor_rows, w_cross_kv, preferred_element_type=jnp.float32).astype(jnp.bfloat16)
    cross_query = jnp.dot(normed, w_cross_q, preferred_element_type=jnp.float32).astype(jnp.bfloat16)
    anchor_mask = jnp.ones((ANCHORS,), bool)

    def one_group(group_query):
        return attend(group_query, anchor_kv[:, :model_width], anchor_kv[:, model_width:], anchor_mask)
    cross_attn = lax.map(one_group, cross_query.reshape(-1, 4 * BLK, model_width)).reshape(-1, model_width)
    cross_term = jnp.dot(cross_attn, w_cross_out, preferred_element_type=jnp.float32)
    point_block = jnp.arange(POINTS) // BLK
    is_live = point_block % NB_DEV < live_blocks[point_block // NB_DEV]
    return jnp.where(is_live[:, None], block_term + cross_term, 0.0).astype(jnp.bfloat16)
```

```python
import functools

import jax
import jax.numpy as jnp
from jax import lax
from jax.experimental import pallas as pl
from jax.experimental.pallas import tpu as pltpu
from jax.sharding import PartitionSpec as P

HEADS = 12
BLK = 128
HB = 2
PAIR = 128
HALF = 64
LIMIT = 50 * 2**20
NEG = -1e30
F32 = jnp.float32
BF16 = jnp.bfloat16


def params():
    return pltpu.CompilerParams(vmem_limit_bytes=LIMIT)


def cost(flops, nbytes, trans=0):
    return pl.CostEstimate(flops=int(flops), bytes_accessed=int(nbytes), transcendentals=int(trans))


def struct(rows, cols, dtype=BF16):
    return jax.ShapeDtypeStruct((rows, cols), dtype)


def whole(array):
    return pl.BlockSpec(array.shape, lambda *_: (0,) * array.ndim)


def mm(a, b):
    return jnp.dot(a, b, preferred_element_type=F32)


def mm_t(a, b):
    return lax.dot_general(a, b, (((1,), (1,)), ((), ())), preferred_element_type=F32)


def normed_rows(rows, gain):
    floats = rows.astype(F32)
    factor = lax.rsqrt(jnp.mean(floats * floats, axis=-1, keepdims=True) + 1e-06)
    return (floats * factor * gain).astype(BF16)


def pick_kernel(send_ref, index_ref, points_ref, first_ref, second_ref, prev_ref, next_ref):
    rows = points_ref.shape[0]
    anchors = index_ref.shape[1]
    slot = lax.broadcasted_iota(jnp.int32, (rows, anchors), 0)
    chosen = jnp.where(slot == index_ref[...], 1.0, 0.0).astype(BF16)
    picked = lax.dot_general(
        chosen, points_ref[...], (((0,), (0,)), ((), ())), preferred_element_type=F32
    ).astype(BF16)
    first_ref[...] = picked[: anchors // 2]
    second_ref[...] = picked[anchors // 2 :]
    for place in range(HB):
        for base, out_ref in ((0, prev_ref), (HB, next_ref)):
            start = pl.multiple_of(send_ref[base + place] * BLK, BLK)
            out_ref[place * BLK : (place + 1) * BLK, :] = points_ref[pl.ds(start, BLK), :]


def pick(points, send_blocks, anchor_index):
    rows, width = points.shape
    anchors = anchor_index.shape[0]
    index = anchor_index.reshape(1, anchors)
    half = struct(anchors // 2, width)
    side = struct(HB * BLK, width)
    return pl.pallas_call(
        pick_kernel,
        out_shape=(half, half, side, side),
        grid_spec=pltpu.PrefetchScalarGridSpec(
            num_scalar_prefetch=1,
            grid=(1,),
            in_specs=[whole(index), whole(points)],
            out_specs=[whole(half), whole(half), whole(side), whole(side)],
        ),
        compiler_params=params(),
        cost_estimate=cost(2 * anchors * rows * width, 4 * rows * width),
    )(send_blocks, index, points)


def project_kernel(points_ref, gain_ref, wqkv_ref, wcq_ref, queries_ref, table_ref):
    width = points_ref.shape[1]
    normed = normed_rows(points_ref[...], gain_ref[...])
    scale = HALF**-0.5
    queries = mm(normed, wqkv_ref[:, :width]).astype(BF16)
    queries_ref[:, :width] = (queries.astype(F32) * scale).astype(BF16)
    cross = mm(normed, wcq_ref[...]).astype(BF16)
    queries_ref[:, width:] = (cross.astype(F32) * scale).astype(BF16)
    table_ref[...] = mm(normed, wqkv_ref[:, width:]).astype(BF16)


def project(points, gain, w_qkv, w_cross_q, extra_rows):
    rows, width = points.shape
    tile = 256
    return pl.pallas_call(
        project_kernel,
        out_shape=(struct(rows, 2 * width), struct(rows + extra_rows, 2 * width)),
        grid=(rows // tile,),
        in_specs=[
            pl.BlockSpec((tile, width), lambda i: (i, 0)),
            whole(gain),
            whole(w_qkv),
            whole(w_cross_q),
        ],
        out_specs=[
            pl.BlockSpec((tile, 2 * width), lambda i: (i, 0)),
            pl.BlockSpec((tile, 2 * width), lambda i: (i, 0)),
        ],
        compiler_params=params(),
        cost_estimate=cost(2 * rows * width * 4 * width, 20 * rows * width),
    )(points, gain, w_qkv, w_cross_q)


def remote_kernel(low_ref, high_ref, gain_ref, wqkv_ref, _, table_ref):
    width = low_ref.shape[1]
    side = low_ref.shape[0]
    for place, ref in enumerate((low_ref, high_ref)):
        normed = normed_rows(ref[...], gain_ref[...])
        table_ref[place * side : (place + 1) * side, :] = mm(
            normed, wqkv_ref[:, width:]
        ).astype(BF16)


def project_remote(low, high, gain, w_qkv, table, own_rows):
    side, width = low.shape
    return pl.pallas_call(
        remote_kernel,
        out_shape=struct(*table.shape),
        grid=(1,),
        in_specs=[
            whole(low),
            whole(high),
            whole(gain),
            whole(w_qkv),
            pl.BlockSpec(memory_space=pl.ANY),
        ],
        out_specs=pl.BlockSpec((2 * side, 2 * width), lambda i: (own_rows // (2 * side), 0)),
        input_output_aliases={4: 0},
        compiler_params=params(),
        cost_estimate=cost(8 * side * width * width, 8 * side * width),
    )(low, high, gain, w_qkv, table)


def split_heads(rows):
    lane = lax.broadcasted_iota(jnp.int32, rows.shape, 1)
    zero = jnp.zeros_like(rows)
    return jnp.concatenate(
        [jnp.where(lane < HALF, rows, zero), jnp.where(lane >= HALF, rows, zero)], axis=0
    )


def join_heads(both):
    count = both.shape[0] // 2
    lane = lax.broadcasted_iota(jnp.int32, (count, PAIR), 1)
    return jnp.where(lane < HALF, both[:count], both[count:])


def block_kernel(ids_ref, count_ref, live_ref, queries_ref, table_ref, out_ref):
    block = pl.program_id(0)
    slots = ids_ref.shape[0] // count_ref.shape[0]
    width = queries_ref.shape[1]
    count = count_ref[block]
    pairs = jnp.where(block < live_ref[0], (count + 1) // 2, 0)

    @pl.when(pairs == 0)
    def _():
        out_ref[...] = jnp.zeros_like(out_ref)

    for used in range(1, slots // 2 + 1):

        @pl.when(pairs == used)
        def _(used=used):
            starts = [
                pl.multiple_of(ids_ref[block * slots + n] * BLK, BLK) for n in range(2 * used)
            ]
            ones = jnp.ones((2 * used * BLK, PAIR), BF16)
            last = (2 * used - 1) * BLK
            dropped = jnp.where(count == 2 * used, 0.0, NEG)
            for pair in range(width // PAIR):
                at = pair * PAIR
                keys = jnp.concatenate(
                    [table_ref[pl.ds(s, BLK), at : at + PAIR] for s in starts], axis=0
                )
                values = jnp.concatenate(
                    [table_ref[pl.ds(s, BLK), width + at : width + at + PAIR] for s in starts],
                    axis=0,
                )
                query = split_heads(queries_ref[:, at : at + PAIR])
                scores = mm_t(query, keys)
                scores = jnp.concatenate([scores[:, :last], scores[:, last:] + dropped], axis=1)
                top = jnp.max(scores, axis=1, keepdims=True)
                weights = jnp.exp(scores - top).astype(BF16)
                total = mm(weights, jnp.concatenate([values, ones], axis=1))
                out_ref[:, at : at + PAIR] = join_heads(total[:, :PAIR] / total[:, PAIR:]).astype(
                    BF16
                )


def block_attention(queries, table, ids, counts, live):
    rows = queries.shape[0]
    width = queries.shape[1] // 2
    blocks = rows // BLK
    return pl.pallas_call(
        block_kernel,
        out_shape=struct(rows, width),
        grid_spec=pltpu.PrefetchScalarGridSpec(
            num_scalar_prefetch=3,
            grid=(blocks,),
            in_specs=[
                pl.BlockSpec((BLK, width), lambda i, *_: (i, 0)),
                whole(table),
            ],
            out_specs=pl.BlockSpec((BLK, width), lambda i, *_: (i, 0)),
        ),
        compiler_params=params(),
        cost_estimate=cost(4 * 4 * rows * 5 * BLK * width, 8 * rows * width, rows * 5 * BLK * 12),
    )(ids.reshape(-1), counts, live, queries, table)


def anchor_kernel(rows_ref, gain_ref, weight_ref, out_ref):
    normed = normed_rows(rows_ref[...], gain_ref[...])
    out_ref[...] = mm(normed, weight_ref[...]).astype(BF16)


def anchor_project(rows, gain, weight):
    count, width = rows.shape
    tile = 512
    return pl.pallas_call(
        anchor_kernel,
        out_shape=struct(count, 2 * width),
        grid=(count // tile,),
        in_specs=[pl.BlockSpec((tile, width), lambda i: (i, 0)), whole(gain), whole(weight)],
        out_specs=pl.BlockSpec((tile, 2 * width), lambda i: (i, 0)),
        compiler_params=params(),
        cost_estimate=cost(4 * count * width * width, 6 * count * width),
    )(rows, gain, weight)


CHUNK = 256


def sweep(query, keys_ref, values_ref, top, total):
    ones = jnp.ones((CHUNK, PAIR), BF16)
    for start in range(0, keys_ref.shape[0], CHUNK):
        scores = mm_t(query, keys_ref[start : start + CHUNK, :])
        here = jnp.max(scores, axis=1, keepdims=True)
        values = jnp.concatenate([values_ref[start : start + CHUNK, :], ones], axis=1)
        if top is None:
            top = here
            total = mm(jnp.exp(scores - top).astype(BF16), values)
        else:
            later = jnp.maximum(top, here)
            total = total * jnp.exp(top - later) + mm(
                jnp.exp(scores - later).astype(BF16), values
            )
            top = later
    return top, total


def cross_first_kernel(queries_ref, keys_ref, values_ref, top_ref, sum_ref, acc_ref):
    query = split_heads(queries_ref[...])
    top, total = sweep(query, keys_ref, values_ref, None, None)
    top_ref[...] = join_heads(jnp.broadcast_to(top, (query.shape[0], PAIR)))
    sum_ref[...] = join_heads(total[:, PAIR:])
    acc_ref[...] = join_heads(total[:, :PAIR])


def cross_last_kernel(
    live_ref,
    queries_ref,
    keys_ref,
    values_ref,
    top_ref,
    sum_ref,
    acc_ref,
    block_ref,
    wout_ref,
    wcross_ref,
    out_ref,
    held_ref,
):
    pair = pl.program_id(1)
    rows = queries_ref.shape[0]
    query = split_heads(queries_ref[...])
    tops = top_ref[...]
    top = jnp.concatenate([tops[:, :1], tops[:, HALF : HALF + 1]], axis=0)
    state = jnp.concatenate([acc_ref[...], sum_ref[...]], axis=1)
    total = jnp.concatenate([state, state], axis=0)
    top, total = sweep(query, keys_ref, values_ref, top, total)
    held_ref[pair] = join_heads(total[:, :PAIR] / total[:, PAIR:]).astype(BF16)

    @pl.when(pair == pl.num_programs(1) - 1)
    def _():
        cross = jnp.concatenate([held_ref[n] for n in range(held_ref.shape[0])], axis=1)
        mixed = mm(block_ref[...], wout_ref[...]) + mm(cross, wcross_ref[...])
        place = lax.broadcasted_iota(jnp.int32, (rows, 1), 0) + pl.program_id(0) * rows
        out_ref[...] = jnp.where(place // BLK < live_ref[0], mixed, 0.0).astype(BF16)


def cross_first(queries, anchor_kv):
    rows = queries.shape[0]
    width = queries.shape[1] // 2
    count = anchor_kv.shape[0]
    pairs = width // PAIR
    tile = 512
    state = struct(rows, width, F32)
    spec = pl.BlockSpec((tile, PAIR), lambda h, i: (i, h))
    return pl.pallas_call(
        cross_first_kernel,
        out_shape=(state, state, state),
        grid=(pairs, rows // tile),
        in_specs=[
            pl.BlockSpec((tile, PAIR), lambda h, i: (i, pairs + h)),
            pl.BlockSpec((count, PAIR), lambda h, i: (0, h)),
            pl.BlockSpec((count, PAIR), lambda h, i: (0, pairs + h)),
        ],
        out_specs=[spec, spec, spec],
        compiler_params=params(),
        cost_estimate=cost(16 * rows * count * width, 24 * rows * width, 12 * rows * count),
    )(queries, anchor_kv, anchor_kv)


def cross_last(queries, anchor_kv, state, block_attn, w_out, w_cross_out, live):
    rows = queries.shape[0]
    width = queries.shape[1] // 2
    count = anchor_kv.shape[0]
    pairs = width // PAIR
    tile = 512
    spec = pl.BlockSpec((tile, PAIR), lambda i, h, *_: (i, h))
    full = pl.BlockSpec((tile, width), lambda i, h, *_: (i, 0))
    return pl.pallas_call(
        cross_last_kernel,
        out_shape=struct(rows, width),
        grid_spec=pltpu.PrefetchScalarGridSpec(
            num_scalar_prefetch=1,
            grid=(rows // tile, pairs),
            in_specs=[
                pl.BlockSpec((tile, PAIR), lambda i, h, *_: (i, pairs + h)),
                pl.BlockSpec((count, PAIR), lambda i, h, *_: (0, h)),
                pl.BlockSpec((count, PAIR), lambda i, h, *_: (0, pairs + h)),
                spec,
                spec,
                spec,
                full,
                whole(w_out),
                whole(w_cross_out),
            ],
            out_specs=full,
            scratch_shapes=[pltpu.VMEM((pairs, tile, PAIR), BF16)],
        ),
        compiler_params=params(),
        cost_estimate=cost(16 * rows * count * width, 24 * rows * width, 12 * rows * count),
    )(live, queries, anchor_kv, anchor_kv, *state, block_attn, w_out, w_cross_out)


def local(
    points,
    norm_gain,
    w_qkv,
    w_out,
    w_cross_q,
    w_cross_kv,
    w_cross_out,
    live_blocks,
    send_blocks,
    neighbours,
    neighbour_count,
    anchor_index,
):
    rows, width = points.shape
    gain = norm_gain.reshape(1, width)
    first, second, to_prev, to_next = pick(points, send_blocks, anchor_index)
    size = lax.axis_size("dom")
    forward = [(i, i + 1) for i in range(size - 1)]
    backward = [(i + 1, i) for i in range(size - 1)]
    low = lax.ppermute(to_next, "dom", forward)
    high = lax.ppermute(to_prev, "dom", backward)
    first = lax.all_gather(first, "dom", axis=0, tiled=True)
    second = lax.all_gather(second, "dom", axis=0, tiled=True)
    queries, table = project(points, gain, w_qkv, w_cross_q, 2 * HB * BLK)
    table = project_remote(low, high, gain, w_qkv, table, rows)
    block_attn = block_attention(queries, table, neighbours, neighbour_count, live_blocks)
    state = cross_first(queries, anchor_project(first, gain, w_cross_kv))
    return cross_last(
        queries,
        anchor_project(second, gain, w_cross_kv),
        state,
        block_attn,
        w_out,
        w_cross_out,
        live_blocks,
    )


def solution(mesh):
    sharded = P(("car", "dom"))
    in_specs = (
        P(("car", "dom"), None),
        P(),
        P(),
        P(),
        P(),
        P(),
        P(),
        sharded,
        sharded,
        P(("car", "dom"), None),
        sharded,
        sharded,
    )
    out_specs = P(("car", "dom"), None)
    return jax.shard_map(local, mesh=mesh, in_specs=in_specs, out_specs=out_specs, check_vma=False)
```

```python
import functools

import jax
import jax.numpy as jnp
from jax import lax
from jax.experimental import pallas as pl
from jax.experimental.pallas import tpu as pltpu
from jax.sharding import PartitionSpec as P

HEADS = 12
BLK = 128
HB = 2
PAIR = 128
HALF = 64
CHUNK = 256
SCALE = HALF**-0.5 * 1.4426950408889634
LIMIT = 32 * 2**20
NEG = -1e30
F32 = jnp.float32
BF16 = jnp.bfloat16


def params():
    return pltpu.CompilerParams(vmem_limit_bytes=LIMIT)


def cost(flops, nbytes, trans=0):
    return pl.CostEstimate(flops=int(flops), bytes_accessed=int(nbytes), transcendentals=int(trans))


def struct(rows, cols, dtype=BF16):
    return jax.ShapeDtypeStruct((rows, cols), dtype)


def whole(array):
    return pl.BlockSpec(array.shape, lambda *_: (0,) * array.ndim)


def mm(a, b):
    return jnp.dot(a, b, preferred_element_type=F32)


def mm_t(a, b):
    return lax.dot_general(a, b, (((1,), (1,)), ((), ())), preferred_element_type=F32)


def normed_rows(rows, gain):
    floats = rows.astype(F32)
    factor = lax.rsqrt(jnp.mean(floats * floats, axis=-1, keepdims=True) + 1e-06)
    return (floats * factor * gain).astype(BF16)


def pick_kernel(send_ref, index_ref, points_ref, anchor_ref, prev_ref, next_ref):
    rows = points_ref.shape[0]
    anchors = index_ref.shape[1]
    slot = lax.broadcasted_iota(jnp.int32, (rows, anchors), 0)
    chosen = jnp.where(slot == index_ref[...], 1.0, 0.0).astype(BF16)
    anchor_ref[...] = lax.dot_general(
        chosen, points_ref[...], (((0,), (0,)), ((), ())), preferred_element_type=F32
    ).astype(BF16)
    for place in range(HB):
        for base, out_ref in ((0, prev_ref), (HB, next_ref)):
            start = pl.multiple_of(send_ref[base + place] * BLK, BLK)
            out_ref[place * BLK : (place + 1) * BLK, :] = points_ref[pl.ds(start, BLK), :]


def pick(points, send_blocks, anchor_index):
    rows, width = points.shape
    anchors = anchor_index.shape[0]
    index = anchor_index.reshape(1, anchors)
    own = struct(anchors, width)
    side = struct(HB * BLK, width)
    return pl.pallas_call(
        pick_kernel,
        out_shape=(own, side, side),
        grid_spec=pltpu.PrefetchScalarGridSpec(
            num_scalar_prefetch=1,
            grid=(1,),
            in_specs=[whole(index), whole(points)],
            out_specs=[whole(own), whole(side), whole(side)],
        ),
        compiler_params=params(),
        cost_estimate=cost(2 * anchors * rows * width, 4 * rows * width),
    )(send_blocks, index, points)


def project_kernel(points_ref, gain_ref, wqkv_ref, wcq_ref, out_ref, normed_ref):
    step = pl.program_id(0)
    rows = points_ref.shape[0]
    tile = rows // 4

    @pl.when(step == 0)
    def _():
        for at in range(0, rows, tile):
            normed = normed_rows(points_ref[at : at + tile, :], gain_ref[...])
            normed_ref[at : at + tile, :] = normed
            out_ref[at : at + tile, :] = (mm(normed, wqkv_ref[...]) * SCALE).astype(BF16)

    @pl.when((step == 1) | (step == 2))
    def _():
        out_ref[...] = mm(normed_ref[...], wqkv_ref[...]).astype(BF16)

    @pl.when(step == 3)
    def _():
        out_ref[...] = (mm(normed_ref[...], wcq_ref[...]) * SCALE).astype(BF16)


def project(points, gain, w_qkv, w_cross_q):
    rows, width = points.shape
    return pl.pallas_call(
        project_kernel,
        out_shape=struct(rows, 4 * width),
        grid=(4,),
        in_specs=[
            whole(points),
            whole(gain),
            pl.BlockSpec((width, width), lambda i: (0, jnp.minimum(i, 2))),
            whole(w_cross_q),
        ],
        out_specs=pl.BlockSpec((rows, width), lambda i: (0, i)),
        scratch_shapes=[pltpu.VMEM((rows, width), BF16)],
        compiler_params=params(),
        cost_estimate=cost(2 * rows * width * 4 * width, 20 * rows * width),
    )(points, gain, w_qkv, w_cross_q)


def split_heads(rows):
    lane = lax.broadcasted_iota(jnp.int32, rows.shape, 1)
    zero = jnp.zeros_like(rows)
    return jnp.concatenate(
        [jnp.where(lane < HALF, rows, zero), jnp.where(lane >= HALF, rows, zero)], axis=0
    )


def join_heads(both):
    count = both.shape[0] // 2
    lane = lax.broadcasted_iota(jnp.int32, (count, PAIR), 1)
    return jnp.where(lane < HALF, both[:count], both[count:])


def weigh(weights, values):
    ones = jnp.ones((values.shape[0], PAIR), BF16)
    return mm(weights.astype(BF16), jnp.concatenate([values, ones], axis=1))


def block_kernel(
    ids_ref,
    count_ref,
    live_ref,
    queries_ref,
    projected_ref,
    low_ref,
    high_ref,
    gain_ref,
    wk_ref,
    wv_ref,
    out_ref,
    table_ref,
    sems,
):
    block = pl.program_id(0)
    slots = ids_ref.shape[1]
    rows = projected_ref.shape[0]
    side, width = low_ref.shape

    @pl.when(block == 0)
    def _():
        copies = [
            pltpu.make_async_copy(
                projected_ref.at[:, (1 + n) * width : (2 + n) * width],
                table_ref.at[n, :rows],
                sems.at[n],
            )
            for n in range(2)
        ]
        for copy in copies:
            copy.start()
        for place, ref in enumerate((low_ref, high_ref)):
            normed = normed_rows(ref[...], gain_ref[...])
            at = rows + place * side
            table_ref[0, at : at + side, :] = mm(normed, wk_ref[...]).astype(BF16)
            table_ref[1, at : at + side, :] = mm(normed, wv_ref[...]).astype(BF16)
        for copy in copies:
            copy.wait()

    count = count_ref[block]
    pairs = jnp.where(block < live_ref[0], (count + 1) // 2, 0)

    @pl.when(pairs == 0)
    def _():
        out_ref[...] = jnp.zeros_like(out_ref)

    for used in range(1, slots // 2 + 1):

        @pl.when(pairs == used)
        def _(used=used):
            starts = [pl.multiple_of(ids_ref[block, n] * BLK, BLK) for n in range(2 * used)]
            dropped = jnp.where(count == 2 * used, 0.0, NEG)

            def rows_of(which, part, at):
                return jnp.concatenate(
                    [
                        table_ref[which, pl.ds(start, BLK), at : at + PAIR]
                        for start in starts[2 * part : 2 * part + 2]
                    ],
                    axis=0,
                )

            for at in range(0, width, PAIR):
                query = split_heads(queries_ref[:, at : at + PAIR])
                scores = [mm_t(query, rows_of(0, part, at)) for part in range(used)]
                last = scores[-1]
                scores[-1] = jnp.concatenate([last[:, :BLK], last[:, BLK:] + dropped], axis=1)
                top = functools.reduce(jnp.maximum, scores)
                top = jnp.max(top, axis=1, keepdims=True)
                total = sum(
                    weigh(jnp.exp2(scores[part] - top), rows_of(1, part, at))
                    for part in range(used)
                )
                out_ref[:, at : at + PAIR] = join_heads(total[:, :PAIR] / total[:, PAIR:]).astype(
                    BF16
                )


def block_attention(projected, low, high, gain, w_qkv, ids, counts, live):
    rows = projected.shape[0]
    width = low.shape[1]
    side = low.shape[0]
    blocks = rows // BLK
    return pl.pallas_call(
        block_kernel,
        out_shape=struct(rows, width),
        grid_spec=pltpu.PrefetchScalarGridSpec(
            num_scalar_prefetch=3,
            grid=(blocks,),
            in_specs=[
                pl.BlockSpec((BLK, width), lambda i, *_: (i, 0)),
                pl.BlockSpec(memory_space=pl.ANY),
                whole(low),
                whole(high),
                whole(gain),
                pl.BlockSpec((width, width), lambda i, *_: (0, 1)),
                pl.BlockSpec((width, width), lambda i, *_: (0, 2)),
            ],
            out_specs=pl.BlockSpec((BLK, width), lambda i, *_: (i, 0)),
            scratch_shapes=[
                pltpu.VMEM((2, rows + 2 * side, width), BF16),
                pltpu.SemaphoreType.DMA((2,)),
            ],
        ),
        compiler_params=params(),
        cost_estimate=cost(16 * rows * 5 * BLK * width, 12 * rows * width, rows * 5 * BLK * 12),
    )(ids, counts, live, projected, projected, low, high, gain, w_qkv, w_qkv)


def anchor_kernel(*refs):
    gain_ref, weight_ref, out_ref = refs[-3:]
    for part, rows_ref in enumerate(refs[:-3]):

        @pl.when(pl.program_id(0) == part)
        def _(rows_ref=rows_ref):
            tile = CHUNK
            for at in range(0, rows_ref.shape[0], tile):
                normed = normed_rows(rows_ref[at : at + tile, :], gain_ref[...])
                out_ref[at : at + tile, :] = mm(normed, weight_ref[...]).astype(BF16)


def anchor_project(parts, gain, weight):
    count, width = parts[0].shape
    every = len(parts) * count
    return pl.pallas_call(
        anchor_kernel,
        out_shape=struct(every, 2 * width),
        grid=(len(parts),),
        in_specs=[whole(part) for part in parts] + [whole(gain), whole(weight)],
        out_specs=pl.BlockSpec((count, 2 * width), lambda i: (i, 0)),
        compiler_params=params(),
        cost_estimate=cost(4 * every * width * width, 6 * every * width),
    )(*parts, gain, weight)


def sweep(query, parts):
    top, total = None, None
    for keys_ref, values_ref in parts:
        for start in range(0, keys_ref.shape[0], CHUNK):
            scores = mm_t(query, keys_ref[start : start + CHUNK, :])
            values = values_ref[start : start + CHUNK, :]
            here = jnp.max(scores, axis=1, keepdims=True)
            if top is None:
                top = here
                total = weigh(jnp.exp2(scores - top), values)
            else:
                later = jnp.maximum(top, here)
                total = total * jnp.exp2(top - later) + weigh(jnp.exp2(scores - later), values)
                top = later
    sums = total[:, PAIR:]
    return join_heads(total[:, :PAIR] / sums), join_heads(top + jnp.log2(sums))


def cross_kernel(queries_ref, keys_ref, values_ref, mean_ref, size_ref):
    query = split_heads(queries_ref[...])
    mean_ref[...], size_ref[...] = sweep(query, [(keys_ref, values_ref)])


def cross_part(projected, anchor_kv):
    rows = projected.shape[0]
    width = projected.shape[1] // 4
    count = anchor_kv.shape[0]
    pairs = width // PAIR
    tile = 512
    state = struct(rows, width, F32)
    spec = pl.BlockSpec((tile, PAIR), lambda h, i: (i, h))
    return pl.pallas_call(
        cross_kernel,
        out_shape=(state, state),
        grid=(pairs, rows // tile),
        in_specs=[
            pl.BlockSpec((tile, PAIR), lambda h, i: (i, 3 * pairs + h)),
            pl.BlockSpec((count, PAIR), lambda h, i: (0, h)),
            pl.BlockSpec((count, PAIR), lambda h, i: (0, pairs + h)),
        ],
        out_specs=[spec, spec],
        compiler_params=params(),
        cost_estimate=cost(16 * rows * count * width, 20 * rows * width, 12 * rows * count),
    )(projected, anchor_kv, anchor_kv)


def final_kernel(
    live_ref,
    queries_ref,
    keys_a_ref,
    values_a_ref,
    keys_b_ref,
    values_b_ref,
    mean_a_ref,
    size_a_ref,
    mean_b_ref,
    size_b_ref,
    block_ref,
    wout_ref,
    wcross_ref,
    out_ref,
    held_ref,
):
    pair = pl.program_id(1)
    rows = queries_ref.shape[0]
    query = split_heads(queries_ref[...])
    mean, size = sweep(query, [(keys_a_ref, values_a_ref), (keys_b_ref, values_b_ref)])
    found = [(mean, size), (mean_a_ref[...], size_a_ref[...]), (mean_b_ref[...], size_b_ref[...])]
    top = functools.reduce(jnp.maximum, [size for _, size in found])
    shares = [jnp.exp2(size - top) for _, size in found]
    joined = sum(mean * share for (mean, _), share in zip(found, shares)) / sum(shares)
    held_ref[pair] = joined.astype(BF16)

    @pl.when(pair == pl.num_programs(1) - 1)
    def _():
        cross = jnp.concatenate([held_ref[n] for n in range(held_ref.shape[0])], axis=1)
        mixed = mm(block_ref[...], wout_ref[...]) + mm(cross, wcross_ref[...])
        place = lax.broadcasted_iota(jnp.int32, (rows, 1), 0) + pl.program_id(0) * rows
        out_ref[...] = jnp.where(place // BLK < live_ref[0], mixed, 0.0).astype(BF16)


def finish(projected, kv_a, kv_b, state_a, state_b, block_attn, w_out, w_cross_out, live):
    rows = projected.shape[0]
    width = projected.shape[1] // 4
    count = kv_a.shape[0]
    pairs = width // PAIR
    tile = 512
    spec = pl.BlockSpec((tile, PAIR), lambda i, h, *_: (i, h))
    full = pl.BlockSpec((tile, width), lambda i, h, *_: (i, 0))
    keys = pl.BlockSpec((count, PAIR), lambda i, h, *_: (0, h))
    values = pl.BlockSpec((count, PAIR), lambda i, h, *_: (0, pairs + h))
    return pl.pallas_call(
        final_kernel,
        out_shape=struct(rows, width),
        grid_spec=pltpu.PrefetchScalarGridSpec(
            num_scalar_prefetch=1,
            grid=(rows // tile, pairs),
            in_specs=[
                pl.BlockSpec((tile, PAIR), lambda i, h, *_: (i, 3 * pairs + h)),
                keys,
                values,
                keys,
                values,
                spec,
                spec,
                spec,
                spec,
                full,
                whole(w_out),
                whole(w_cross_out),
            ],
            out_specs=full,
            scratch_shapes=[pltpu.VMEM((pairs, tile, PAIR), BF16)],
        ),
        compiler_params=params(),
        cost_estimate=cost(32 * rows * count * width, 40 * rows * width, 24 * rows * count),
    )(live, projected, kv_a, kv_a, kv_b, kv_b, *state_a, *state_b, block_attn, w_out, w_cross_out)


def after(*arrays):
    return lax.optimization_barrier(arrays)


def permute(array, target):
    size = lax.axis_size("dom")
    pairs = [(i, target(i)) for i in range(size) if 0 <= target(i) < size]
    return lax.ppermute(array, "dom", pairs)


def local(
    points,
    norm_gain,
    w_qkv,
    w_out,
    w_cross_q,
    w_cross_kv,
    w_cross_out,
    live_blocks,
    send_blocks,
    neighbours,
    neighbour_count,
    anchor_index,
):
    rows, width = points.shape
    gain = norm_gain.reshape(1, width)
    size = lax.axis_size("dom")
    column, ring = 2, 4
    anchors, to_prev, to_next = pick(points, send_blocks, anchor_index)
    beside = permute(anchors, lambda i: i ^ column)
    low = permute(to_next, lambda i: i + 1)
    high = permute(to_prev, lambda i: i - 1)
    points, anchors = after(points, anchors)
    projected = project(points, gain, w_qkv, w_cross_q)
    beside, projected = after(beside, projected)
    near = jnp.concatenate([anchors, beside], axis=0)
    above = permute(near, lambda i: (i + ring) % size)
    below = permute(near, lambda i: (i - ring) % size)
    block_attn = block_attention(
        projected, low, high, gain, w_qkv, neighbours, neighbour_count, live_blocks
    )
    near, above, below, block_attn = after(near, above, below, block_attn)
    far = permute(near, lambda i: (i + 2 * ring) % size)
    kv_a = anchor_project([near, above, below], gain, w_cross_kv)
    kv_a_other = permute(kv_a, lambda i: i ^ 1)
    state_a = cross_part(projected, kv_a)
    far, state_a = after(far, state_a)
    kv_b = anchor_project([far], gain, w_cross_kv)
    kv_b, kv_a_other = after(kv_b, kv_a_other)
    kv_b_other = permute(kv_b, lambda i: i ^ 1)
    state_b = cross_part(projected, kv_a_other)
    return finish(
        projected, kv_b, kv_b_other, state_a, state_b, block_attn, w_out, w_cross_out, live_blocks
    )


def solution(mesh):
    sharded = P(("car", "dom"))
    in_specs = (
        P(("car", "dom"), None),
        P(),
        P(),
        P(),
        P(),
        P(),
        P(),
        sharded,
        sharded,
        P(("car", "dom"), None),
        sharded,
        sharded,
    )
    out_specs = P(("car", "dom"), None)
    return jax.shard_map(local, mesh=mesh, in_specs=in_specs, out_specs=out_specs, check_vma=False)
```

```python
import functools

import jax
import jax.numpy as jnp
from jax import lax
from jax.experimental import pallas as pl
from jax.experimental.pallas import tpu as pltpu
from jax.sharding import PartitionSpec as P

HEADS = 12
BLK = 128
HB = 2
PAIR = 128
HALF = 64
CHUNK = 256
SCALE = HALF**-0.5 * 1.4426950408889634
LIMIT = 32 * 2**20
WIDE = 61 * 2**20
NEG = -1e30
F32 = jnp.float32
BF16 = jnp.bfloat16


def params(limit=LIMIT):
    return pltpu.CompilerParams(vmem_limit_bytes=limit)


def cost(flops, nbytes, trans=0):
    return pl.CostEstimate(flops=int(flops), bytes_accessed=int(nbytes), transcendentals=int(trans))


def struct(rows, cols, dtype=BF16):
    return jax.ShapeDtypeStruct((rows, cols), dtype)


def whole(array):
    return pl.BlockSpec(array.shape, lambda *_: (0,) * array.ndim)


def mm(a, b):
    return jnp.dot(a, b, preferred_element_type=F32)


def mm_t(a, b):
    return lax.dot_general(a, b, (((1,), (1,)), ((), ())), preferred_element_type=F32)


def normed_rows(rows, gain):
    floats = rows.astype(F32)
    factor = lax.rsqrt(jnp.mean(floats * floats, axis=-1, keepdims=True) + 1e-06)
    return (floats * factor * gain).astype(BF16)


def pick_kernel(send_ref, index_ref, source_ref, anchor_ref, prev_ref, next_ref, points_ref, sem):
    copy = pltpu.make_async_copy(source_ref, points_ref, sem)
    copy.start()
    rows = points_ref.shape[0]
    anchors = index_ref.shape[1]
    slot = lax.broadcasted_iota(jnp.int32, (rows, anchors), 0)
    chosen = jnp.where(slot == index_ref[...], 1.0, 0.0).astype(BF16)
    copy.wait()
    anchor_ref[...] = lax.dot_general(
        chosen, points_ref[...], (((0,), (0,)), ((), ())), preferred_element_type=F32
    ).astype(BF16)
    for place in range(HB):
        for base, out_ref in ((0, prev_ref), (HB, next_ref)):
            start = pl.multiple_of(send_ref[base + place] * BLK, BLK)
            out_ref[place * BLK : (place + 1) * BLK, :] = points_ref[pl.ds(start, BLK), :]


def pick(points, send_blocks, anchor_index):
    rows, width = points.shape
    anchors = anchor_index.shape[0]
    index = anchor_index.reshape(1, anchors)
    own = struct(anchors, width)
    side = struct(HB * BLK, width)
    return pl.pallas_call(
        pick_kernel,
        out_shape=(own, side, side),
        in_specs=[
            pl.BlockSpec(memory_space=pltpu.SMEM),
            pl.BlockSpec(memory_space=pltpu.VMEM),
            pl.BlockSpec(memory_space=pltpu.HBM),
        ],
        scratch_shapes=[pltpu.VMEM((rows, width), BF16), pltpu.SemaphoreType.DMA],
        compiler_params=params(WIDE),
        cost_estimate=cost(2 * anchors * rows * width, 4 * rows * width),
    )(send_blocks, index, points)


def project_kernel(
    source_ref, gain_ref, wqkv_ref, wcq_ref, out_ref, points_ref, weight_ref, held_ref, sems
):
    rows, width = points_ref.shape
    tile = rows // 4
    fetches = [pltpu.make_async_copy(source_ref, points_ref, sems.at[0])]
    for n in range(4):
        part = wcq_ref if n == 3 else wqkv_ref.at[:, n * width : (n + 1) * width]
        fetches.append(pltpu.make_async_copy(part, weight_ref.at[n], sems.at[1 + n]))
    for fetch in fetches:
        fetch.start()
    fetches[0].wait()
    stores = []
    for n in range(4):
        slot = n % 2
        if n >= 2:
            stores[n - 2].wait()
        for at in range(0, rows, tile):
            if n == 0:
                points_ref[at : at + tile, :] = normed_rows(
                    points_ref[at : at + tile, :], gain_ref[...]
                )
            if at == 0:
                fetches[1 + n].wait()
            made = mm(points_ref[at : at + tile, :], weight_ref[n])
            if n == 0 or n == 3:
                made = made * SCALE
            held_ref[slot, at : at + tile, :] = made.astype(BF16)
        store = pltpu.make_async_copy(
            held_ref.at[slot], out_ref.at[:, n * width : (n + 1) * width], sems.at[5 + slot]
        )
        store.start()
        stores.append(store)
    stores[2].wait()
    stores[3].wait()


def project(points, gain, w_qkv, w_cross_q):
    rows, width = points.shape
    hbm = pl.BlockSpec(memory_space=pltpu.HBM)
    return pl.pallas_call(
        project_kernel,
        out_shape=struct(rows, 4 * width),
        in_specs=[hbm, pl.BlockSpec(memory_space=pltpu.VMEM), hbm, hbm],
        out_specs=hbm,
        scratch_shapes=[
            pltpu.VMEM((rows, width), BF16),
            pltpu.VMEM((4, width, width), BF16),
            pltpu.VMEM((2, rows, width), BF16),
            pltpu.SemaphoreType.DMA((7,)),
        ],
        compiler_params=params(WIDE),
        cost_estimate=cost(2 * rows * width * 4 * width, 20 * rows * width),
    )(points, gain, w_qkv, w_cross_q)


def split_heads(rows):
    lane = lax.broadcasted_iota(jnp.int32, rows.shape, 1)
    zero = jnp.zeros_like(rows)
    return jnp.concatenate(
        [jnp.where(lane < HALF, rows, zero), jnp.where(lane >= HALF, rows, zero)], axis=0
    )


def join_heads(both):
    count = both.shape[0] // 2
    lane = lax.broadcasted_iota(jnp.int32, (count, PAIR), 1)
    return jnp.where(lane < HALF, both[:count], both[count:])


def weigh(weights, values):
    ones = jnp.ones((values.shape[0], PAIR), BF16)
    return mm(weights.astype(BF16), jnp.concatenate([values, ones], axis=1))


def block_kernel(
    ids_ref,
    count_ref,
    live_ref,
    queries_ref,
    projected_ref,
    low_ref,
    high_ref,
    gain_ref,
    wk_ref,
    wv_ref,
    out_ref,
    table_ref,
    sems,
):
    block = pl.program_id(0)
    slots = ids_ref.shape[1]
    rows = projected_ref.shape[0]
    side, width = low_ref.shape

    @pl.when(block == 0)
    def _():
        copies = [
            pltpu.make_async_copy(
                projected_ref.at[:, (1 + n) * width : (2 + n) * width],
                table_ref.at[n, :rows],
                sems.at[n],
            )
            for n in range(2)
        ]
        for copy in copies:
            copy.start()
        for place, ref in enumerate((low_ref, high_ref)):
            normed = normed_rows(ref[...], gain_ref[...])
            at = rows + place * side
            table_ref[0, at : at + side, :] = mm(normed, wk_ref[...]).astype(BF16)
            table_ref[1, at : at + side, :] = mm(normed, wv_ref[...]).astype(BF16)
        for copy in copies:
            copy.wait()

    count = count_ref[block]
    pairs = jnp.where(block < live_ref[0], (count + 1) // 2, 0)

    @pl.when(pairs == 0)
    def _():
        out_ref[...] = jnp.zeros_like(out_ref)

    for used in range(1, slots // 2 + 1):

        @pl.when(pairs == used)
        def _(used=used):
            starts = [pl.multiple_of(ids_ref[block, n] * BLK, BLK) for n in range(2 * used)]
            dropped = jnp.where(count == 2 * used, 0.0, NEG)

            def rows_of(which, part, at):
                return jnp.concatenate(
                    [
                        table_ref[which, pl.ds(start, BLK), at : at + PAIR]
                        for start in starts[2 * part : 2 * part + 2]
                    ],
                    axis=0,
                )

            for at in range(0, width, PAIR):
                query = split_heads(queries_ref[:, at : at + PAIR])
                scores = [mm_t(query, rows_of(0, part, at)) for part in range(used)]
                last = scores[-1]
                scores[-1] = jnp.concatenate([last[:, :BLK], last[:, BLK:] + dropped], axis=1)
                top = functools.reduce(jnp.maximum, scores)
                top = jnp.max(top, axis=1, keepdims=True)
                total = sum(
                    weigh(jnp.exp2(scores[part] - top), rows_of(1, part, at))
                    for part in range(used)
                )
                out_ref[:, at : at + PAIR] = join_heads(total[:, :PAIR] / total[:, PAIR:]).astype(
                    BF16
                )


def block_attention(projected, low, high, gain, w_qkv, ids, counts, live):
    rows = projected.shape[0]
    width = low.shape[1]
    side = low.shape[0]
    blocks = rows // BLK
    return pl.pallas_call(
        block_kernel,
        out_shape=struct(rows, width),
        grid_spec=pltpu.PrefetchScalarGridSpec(
            num_scalar_prefetch=3,
            grid=(blocks,),
            in_specs=[
                pl.BlockSpec((BLK, width), lambda i, *_: (i, 0)),
                pl.BlockSpec(memory_space=pl.ANY),
                whole(low),
                whole(high),
                whole(gain),
                pl.BlockSpec((width, width), lambda i, *_: (0, 1)),
                pl.BlockSpec((width, width), lambda i, *_: (0, 2)),
            ],
            out_specs=pl.BlockSpec((BLK, width), lambda i, *_: (i, 0)),
            scratch_shapes=[
                pltpu.VMEM((2, rows + 2 * side, width), BF16),
                pltpu.SemaphoreType.DMA((2,)),
            ],
        ),
        compiler_params=params(WIDE),
        cost_estimate=cost(16 * rows * 5 * BLK * width, 12 * rows * width, rows * 5 * BLK * 12),
    )(ids, counts, live, projected, projected, low, high, gain, w_qkv, w_qkv)


def anchor_kernel(*refs):
    gain_ref, weight_ref, out_ref = refs[-3:]
    for part, rows_ref in enumerate(refs[:-3]):

        @pl.when(pl.program_id(0) == part)
        def _(rows_ref=rows_ref):
            tile = CHUNK
            for at in range(0, rows_ref.shape[0], tile):
                normed = normed_rows(rows_ref[at : at + tile, :], gain_ref[...])
                out_ref[at : at + tile, :] = mm(normed, weight_ref[...]).astype(BF16)


def anchor_project(parts, gain, weight):
    count, width = parts[0].shape
    every = len(parts) * count
    return pl.pallas_call(
        anchor_kernel,
        out_shape=struct(every, 2 * width),
        grid=(len(parts),),
        in_specs=[whole(part) for part in parts] + [whole(gain), whole(weight)],
        out_specs=pl.BlockSpec((count, 2 * width), lambda i: (i, 0)),
        compiler_params=params(),
        cost_estimate=cost(4 * every * width * width, 6 * every * width),
    )(*parts, gain, weight)


def sweep(query, parts):
    top, total = None, None
    for keys_ref, values_ref in parts:
        for start in range(0, keys_ref.shape[0], CHUNK):
            scores = mm_t(query, keys_ref[start : start + CHUNK, :])
            values = values_ref[start : start + CHUNK, :]
            here = jnp.max(scores, axis=1, keepdims=True)
            if top is None:
                top = here
                total = weigh(jnp.exp2(scores - top), values)
            else:
                later = jnp.maximum(top, here)
                total = total * jnp.exp2(top - later) + weigh(jnp.exp2(scores - later), values)
                top = later
    sums = total[:, PAIR:]
    return join_heads(total[:, :PAIR] / sums), join_heads(top + jnp.log2(sums))


def cross_kernel(queries_ref, keys_ref, values_ref, mean_ref, size_ref):
    query = split_heads(queries_ref[...])
    mean_ref[...], size_ref[...] = sweep(query, [(keys_ref, values_ref)])


def cross_part(projected, anchor_kv):
    rows = projected.shape[0]
    width = projected.shape[1] // 4
    count = anchor_kv.shape[0]
    pairs = width // PAIR
    tile = 512
    state = struct(rows, width, F32)
    spec = pl.BlockSpec((tile, PAIR), lambda h, i: (i, h))
    return pl.pallas_call(
        cross_kernel,
        out_shape=(state, state),
        grid=(pairs, rows // tile),
        in_specs=[
            pl.BlockSpec((tile, PAIR), lambda h, i: (i, 3 * pairs + h)),
            pl.BlockSpec((count, PAIR), lambda h, i: (0, h)),
            pl.BlockSpec((count, PAIR), lambda h, i: (0, pairs + h)),
        ],
        out_specs=[spec, spec],
        compiler_params=params(WIDE),
        cost_estimate=cost(16 * rows * count * width, 20 * rows * width, 12 * rows * count),
    )(projected, anchor_kv, anchor_kv)


def final_kernel(
    live_ref,
    queries_ref,
    keys_a_ref,
    values_a_ref,
    keys_b_ref,
    values_b_ref,
    mean_ref,
    size_ref,
    block_ref,
    wout_ref,
    wcross_ref,
    out_ref,
    held_ref,
):
    pair = pl.program_id(1)
    rows = queries_ref.shape[0]
    query = split_heads(queries_ref[...])
    mean, size = sweep(query, [(keys_a_ref, values_a_ref), (keys_b_ref, values_b_ref)])
    top = jnp.maximum(size, size_ref[...])
    share, other = jnp.exp2(size - top), jnp.exp2(size_ref[...] - top)
    held_ref[pair] = ((mean * share + mean_ref[...] * other) / (share + other)).astype(BF16)

    @pl.when(pair == pl.num_programs(1) - 1)
    def _():
        cross = jnp.concatenate([held_ref[n] for n in range(held_ref.shape[0])], axis=1)
        mixed = mm(block_ref[...], wout_ref[...]) + mm(cross, wcross_ref[...])
        place = lax.broadcasted_iota(jnp.int32, (rows, 1), 0) + pl.program_id(0) * rows
        out_ref[...] = jnp.where(place // BLK < live_ref[0], mixed, 0.0).astype(BF16)


def finish(projected, kv_a, kv_b, state, block_attn, w_out, w_cross_out, live):
    rows = projected.shape[0]
    width = projected.shape[1] // 4
    count = kv_a.shape[0] + kv_b.shape[0]
    pairs = width // PAIR
    tile = 512
    spec = pl.BlockSpec((tile, PAIR), lambda i, h, *_: (i, h))
    full = pl.BlockSpec((tile, width), lambda i, h, *_: (i, 0))
    table_specs = []
    for table in (kv_a, kv_b):
        table_specs.append(pl.BlockSpec((table.shape[0], PAIR), lambda i, h, *_: (0, h)))
        table_specs.append(pl.BlockSpec((table.shape[0], PAIR), lambda i, h, *_: (0, pairs + h)))
    return pl.pallas_call(
        final_kernel,
        out_shape=struct(rows, width),
        grid_spec=pltpu.PrefetchScalarGridSpec(
            num_scalar_prefetch=1,
            grid=(rows // tile, pairs),
            in_specs=[
                pl.BlockSpec((tile, PAIR), lambda i, h, *_: (i, 3 * pairs + h)),
                *table_specs,
                spec,
                spec,
                full,
                whole(w_out),
                whole(w_cross_out),
            ],
            out_specs=full,
            scratch_shapes=[pltpu.VMEM((pairs, tile, PAIR), BF16)],
        ),
        compiler_params=params(WIDE),
        cost_estimate=cost(16 * rows * count * width, 28 * rows * width, 12 * rows * count),
    )(live, projected, kv_a, kv_a, kv_b, kv_b, *state, block_attn, w_out, w_cross_out)


def after(*arrays):
    return lax.optimization_barrier(arrays)


def permute(array, target):
    size = lax.axis_size("dom")
    pairs = [(i, target(i)) for i in range(size) if 0 <= target(i) < size]
    return lax.ppermute(array, "dom", pairs)


def local(
    points,
    norm_gain,
    w_qkv,
    w_out,
    w_cross_q,
    w_cross_kv,
    w_cross_out,
    live_blocks,
    send_blocks,
    neighbours,
    neighbour_count,
    anchor_index,
):
    rows, width = points.shape
    gain = norm_gain.reshape(1, width)
    size = lax.axis_size("dom")
    column, ring = 2, 4
    anchors, to_prev, to_next = pick(points, send_blocks, anchor_index)
    beside = permute(anchors, lambda i: i ^ column)
    low = permute(to_next, lambda i: i + 1)
    high = permute(to_prev, lambda i: i - 1)
    points, anchors = after(points, anchors)
    projected = project(points, gain, w_qkv, w_cross_q)
    beside, projected = after(beside, projected)
    near = jnp.concatenate([anchors, beside], axis=0)
    above = permute(near, lambda i: (i + ring) % size)
    below = permute(near, lambda i: (i - ring) % size)
    block_attn = block_attention(
        projected, low, high, gain, w_qkv, neighbours, neighbour_count, live_blocks
    )
    near, above, below, block_attn = after(near, above, below, block_attn)
    kv_a = anchor_project([near, above, below], gain, w_cross_kv)
    kv_a_other = permute(kv_a, lambda i: i ^ 1)
    far = permute(near, lambda i: (i + 2 * ring) % size)
    far_other = permute(near, lambda i: ((i + 2 * ring) % size) ^ 1)
    state = cross_part(projected, kv_a)
    far, far_other, state = after(far, far_other, state)
    kv_b = anchor_project([far, far_other], gain, w_cross_kv)
    return finish(projected, kv_b, kv_a_other, state, block_attn, w_out, w_cross_out, live_blocks)


def solution(mesh):
    sharded = P(("car", "dom"))
    in_specs = (
        P(("car", "dom"), None),
        P(),
        P(),
        P(),
        P(),
        P(),
        P(),
        sharded,
        sharded,
        P(("car", "dom"), None),
        sharded,
        sharded,
    )
    out_specs = P(("car", "dom"), None)
    return jax.shard_map(local, mesh=mesh, in_specs=in_specs, out_specs=out_specs, check_vma=False)
```

```python
import functools

import jax
import jax.numpy as jnp
from jax import lax
from jax.experimental import pallas as pl
from jax.experimental.pallas import tpu as pltpu
from jax.sharding import PartitionSpec as P

HEADS = 12
BLK = 128
HB = 2
PAIR = 128
HALF = 64
CHUNK = 256
SCALE = HALF**-0.5 * 1.4426950408889634
LIMIT = 32 * 2**20
WIDE = 61 * 2**20
NEG = -1e30
F32 = jnp.float32
BF16 = jnp.bfloat16


def params(limit=LIMIT):
    return pltpu.CompilerParams(vmem_limit_bytes=limit)


def cost(flops, nbytes, trans=0):
    return pl.CostEstimate(flops=int(flops), bytes_accessed=int(nbytes), transcendentals=int(trans))


def struct(rows, cols, dtype=BF16):
    return jax.ShapeDtypeStruct((rows, cols), dtype)


def whole(array):
    return pl.BlockSpec(array.shape, lambda *_: (0,) * array.ndim)


def mm(a, b):
    return jnp.dot(a, b, preferred_element_type=F32)


def mm_t(a, b):
    return lax.dot_general(a, b, (((1,), (1,)), ((), ())), preferred_element_type=F32)


def normed_rows(rows, gain):
    floats = rows.astype(F32)
    factor = lax.rsqrt(jnp.mean(floats * floats, axis=-1, keepdims=True) + 1e-06)
    return (floats * factor * gain).astype(BF16)


def pick_kernel(send_ref, index_ref, source_ref, anchor_ref, prev_ref, next_ref, points_ref, sem):
    copy = pltpu.make_async_copy(source_ref, points_ref, sem)
    copy.start()
    rows = points_ref.shape[0]
    anchors = index_ref.shape[1]
    slot = lax.broadcasted_iota(jnp.int32, (rows, anchors), 0)
    chosen = jnp.where(slot == index_ref[...], 1.0, 0.0).astype(BF16)
    copy.wait()
    anchor_ref[...] = lax.dot_general(
        chosen, points_ref[...], (((0,), (0,)), ((), ())), preferred_element_type=F32
    ).astype(BF16)
    for place in range(HB):
        for base, out_ref in ((0, prev_ref), (HB, next_ref)):
            start = pl.multiple_of(send_ref[base + place] * BLK, BLK)
            out_ref[place * BLK : (place + 1) * BLK, :] = points_ref[pl.ds(start, BLK), :]


def pick(points, send_blocks, anchor_index):
    rows, width = points.shape
    anchors = anchor_index.shape[0]
    index = anchor_index.reshape(1, anchors)
    own = struct(anchors, width)
    side = struct(HB * BLK, width)
    return pl.pallas_call(
        pick_kernel,
        out_shape=(own, side, side),
        in_specs=[
            pl.BlockSpec(memory_space=pltpu.SMEM),
            pl.BlockSpec(memory_space=pltpu.VMEM),
            pl.BlockSpec(memory_space=pltpu.HBM),
        ],
        scratch_shapes=[pltpu.VMEM((rows, width), BF16), pltpu.SemaphoreType.DMA],
        compiler_params=params(WIDE),
        cost_estimate=cost(2 * anchors * rows * width, 4 * rows * width),
    )(send_blocks, index, points)


def project_kernel(points_ref, gain_ref, wqkv_ref, wcq_ref, out_ref, normed_ref):
    step = pl.program_id(0)
    rows = points_ref.shape[0]
    tile = rows // 4

    @pl.when(step == 0)
    def _():
        for at in range(0, rows, tile):
            normed = normed_rows(points_ref[at : at + tile, :], gain_ref[...])
            normed_ref[at : at + tile, :] = normed
            out_ref[at : at + tile, :] = (mm(normed, wqkv_ref[...]) * SCALE).astype(BF16)

    @pl.when((step == 1) | (step == 2))
    def _():
        out_ref[...] = mm(normed_ref[...], wqkv_ref[...]).astype(BF16)

    @pl.when(step == 3)
    def _():
        out_ref[...] = (mm(normed_ref[...], wcq_ref[...]) * SCALE).astype(BF16)


def project(points, gain, w_qkv, w_cross_q):
    rows, width = points.shape
    return pl.pallas_call(
        project_kernel,
        out_shape=struct(rows, 4 * width),
        grid=(4,),
        in_specs=[
            whole(points),
            whole(gain),
            pl.BlockSpec((width, width), lambda i: (0, jnp.minimum(i, 2))),
            whole(w_cross_q),
        ],
        out_specs=pl.BlockSpec((rows, width), lambda i: (0, i)),
        scratch_shapes=[pltpu.VMEM((rows, width), BF16)],
        compiler_params=params(),
        cost_estimate=cost(2 * rows * width * 4 * width, 20 * rows * width),
    )(points, gain, w_qkv, w_cross_q)


def split_heads(rows):
    lane = lax.broadcasted_iota(jnp.int32, rows.shape, 1)
    zero = jnp.zeros_like(rows)
    return jnp.concatenate(
        [jnp.where(lane < HALF, rows, zero), jnp.where(lane >= HALF, rows, zero)], axis=0
    )


def join_heads(both):
    count = both.shape[0] // 2
    lane = lax.broadcasted_iota(jnp.int32, (count, PAIR), 1)
    return jnp.where(lane < HALF, both[:count], both[count:])


def weigh(weights, values):
    ones = jnp.ones((values.shape[0], PAIR), BF16)
    return mm(weights.astype(BF16), jnp.concatenate([values, ones], axis=1))


def block_kernel(
    ids_ref,
    count_ref,
    live_ref,
    queries_ref,
    projected_ref,
    low_ref,
    high_ref,
    gain_ref,
    wk_ref,
    wv_ref,
    out_ref,
    table_ref,
    sems,
):
    block = pl.program_id(0)
    slots = ids_ref.shape[1]
    rows = projected_ref.shape[0]
    side, width = low_ref.shape

    @pl.when(block == 0)
    def _():
        copies = [
            pltpu.make_async_copy(
                projected_ref.at[:, (1 + n) * width : (2 + n) * width],
                table_ref.at[n, :rows],
                sems.at[n],
            )
            for n in range(2)
        ]
        for copy in copies:
            copy.start()
        for place, ref in enumerate((low_ref, high_ref)):
            normed = normed_rows(ref[...], gain_ref[...])
            at = rows + place * side
            table_ref[0, at : at + side, :] = mm(normed, wk_ref[...]).astype(BF16)
            table_ref[1, at : at + side, :] = mm(normed, wv_ref[...]).astype(BF16)
        for copy in copies:
            copy.wait()

    count = count_ref[block]
    pairs = jnp.where(block < live_ref[0], (count + 1) // 2, 0)

    @pl.when(pairs == 0)
    def _():
        out_ref[...] = jnp.zeros_like(out_ref)

    for used in range(1, slots // 2 + 1):

        @pl.when(pairs == used)
        def _(used=used):
            starts = [pl.multiple_of(ids_ref[block, n] * BLK, BLK) for n in range(2 * used)]
            dropped = jnp.where(count == 2 * used, 0.0, NEG)

            def rows_of(which, part, at):
                return jnp.concatenate(
                    [
                        table_ref[which, pl.ds(start, BLK), at : at + PAIR]
                        for start in starts[2 * part : 2 * part + 2]
                    ],
                    axis=0,
                )

            for at in range(0, width, PAIR):
                query = split_heads(queries_ref[:, at : at + PAIR])
                scores = [mm_t(query, rows_of(0, part, at)) for part in range(used)]
                last = scores[-1]
                scores[-1] = jnp.concatenate([last[:, :BLK], last[:, BLK:] + dropped], axis=1)
                top = functools.reduce(jnp.maximum, scores)
                top = jnp.max(top, axis=1, keepdims=True)
                total = sum(
                    weigh(jnp.exp2(scores[part] - top), rows_of(1, part, at))
                    for part in range(used)
                )
                out_ref[:, at : at + PAIR] = join_heads(total[:, :PAIR] / total[:, PAIR:]).astype(
                    BF16
                )


def block_attention(projected, low, high, gain, w_qkv, ids, counts, live):
    rows = projected.shape[0]
    width = low.shape[1]
    side = low.shape[0]
    blocks = rows // BLK
    return pl.pallas_call(
        block_kernel,
        out_shape=struct(rows, width),
        grid_spec=pltpu.PrefetchScalarGridSpec(
            num_scalar_prefetch=3,
            grid=(blocks,),
            in_specs=[
                pl.BlockSpec((BLK, width), lambda i, *_: (i, 0)),
                pl.BlockSpec(memory_space=pl.ANY),
                whole(low),
                whole(high),
                whole(gain),
                pl.BlockSpec((width, width), lambda i, *_: (0, 1)),
                pl.BlockSpec((width, width), lambda i, *_: (0, 2)),
            ],
            out_specs=pl.BlockSpec((BLK, width), lambda i, *_: (i, 0)),
            scratch_shapes=[
                pltpu.VMEM((2, rows + 2 * side, width), BF16),
                pltpu.SemaphoreType.DMA((2,)),
            ],
        ),
        compiler_params=params(),
        cost_estimate=cost(16 * rows * 5 * BLK * width, 12 * rows * width, rows * 5 * BLK * 12),
    )(ids, counts, live, projected, projected, low, high, gain, w_qkv, w_qkv)


def anchor_kernel(*refs):
    gain_ref, weight_ref, out_ref = refs[-3:]
    for part, rows_ref in enumerate(refs[:-3]):

        @pl.when(pl.program_id(0) == part)
        def _(rows_ref=rows_ref):
            tile = CHUNK
            for at in range(0, rows_ref.shape[0], tile):
                normed = normed_rows(rows_ref[at : at + tile, :], gain_ref[...])
                out_ref[at : at + tile, :] = mm(normed, weight_ref[...]).astype(BF16)


def anchor_project(parts, gain, weight):
    count, width = parts[0].shape
    every = len(parts) * count
    return pl.pallas_call(
        anchor_kernel,
        out_shape=struct(every, 2 * width),
        grid=(len(parts),),
        in_specs=[whole(part) for part in parts] + [whole(gain), whole(weight)],
        out_specs=pl.BlockSpec((count, 2 * width), lambda i: (i, 0)),
        compiler_params=params(),
        cost_estimate=cost(4 * every * width * width, 6 * every * width),
    )(*parts, gain, weight)


def sweep(query, keys_ref, values_ref):
    top, total = None, None
    for start in range(0, keys_ref.shape[0], CHUNK):
        scores = mm_t(query, keys_ref[start : start + CHUNK, :])
        values = values_ref[start : start + CHUNK, :]
        here = jnp.max(scores, axis=1, keepdims=True)
        if top is None:
            top = here
            total = weigh(jnp.exp2(scores - top), values)
        else:
            later = jnp.maximum(top, here)
            total = total * jnp.exp2(top - later) + weigh(jnp.exp2(scores - later), values)
            top = later
    sums = total[:, PAIR:]
    return join_heads(total[:, :PAIR] / sums), join_heads(top + jnp.log2(sums))


def cross_kernel(queries_ref, keys_ref, values_ref, mean_ref, size_ref):
    query = split_heads(queries_ref[...])
    mean_ref[...], size_ref[...] = sweep(query, keys_ref, values_ref)


def cross_part(projected, anchor_kv):
    rows = projected.shape[0]
    width = projected.shape[1] // 4
    count = anchor_kv.shape[0]
    pairs = width // PAIR
    tile = 512
    state = struct(rows, width, F32)
    spec = pl.BlockSpec((tile, PAIR), lambda h, i: (i, h))
    return pl.pallas_call(
        cross_kernel,
        out_shape=(state, state),
        grid=(pairs, rows // tile),
        in_specs=[
            pl.BlockSpec((tile, PAIR), lambda h, i: (i, 3 * pairs + h)),
            pl.BlockSpec((count, PAIR), lambda h, i: (0, h)),
            pl.BlockSpec((count, PAIR), lambda h, i: (0, pairs + h)),
        ],
        out_specs=[spec, spec],
        compiler_params=params(WIDE),
        cost_estimate=cost(16 * rows * count * width, 20 * rows * width, 12 * rows * count),
    )(projected, anchor_kv, anchor_kv)


def final_kernel(
    live_ref,
    queries_ref,
    keys_ref,
    values_ref,
    mean_ref,
    size_ref,
    block_ref,
    wout_ref,
    wcross_ref,
    out_ref,
    held_ref,
):
    pair = pl.program_id(1)
    rows = queries_ref.shape[0]
    query = split_heads(queries_ref[...])
    mean, size = sweep(query, keys_ref, values_ref)
    top = jnp.maximum(size, size_ref[...])
    share, other = jnp.exp2(size - top), jnp.exp2(size_ref[...] - top)
    held_ref[pair] = ((mean * share + mean_ref[...] * other) / (share + other)).astype(BF16)

    @pl.when(pair == pl.num_programs(1) - 1)
    def _():
        cross = jnp.concatenate([held_ref[n] for n in range(held_ref.shape[0])], axis=1)
        mixed = mm(block_ref[...], wout_ref[...]) + mm(cross, wcross_ref[...])
        place = lax.broadcasted_iota(jnp.int32, (rows, 1), 0) + pl.program_id(0) * rows
        out_ref[...] = jnp.where(place // BLK < live_ref[0], mixed, 0.0).astype(BF16)


def finish(projected, anchor_kv, state, block_attn, w_out, w_cross_out, live):
    rows = projected.shape[0]
    width = projected.shape[1] // 4
    count = anchor_kv.shape[0]
    pairs = width // PAIR
    tile = 512
    spec = pl.BlockSpec((tile, PAIR), lambda i, h, *_: (i, h))
    full = pl.BlockSpec((tile, width), lambda i, h, *_: (i, 0))
    return pl.pallas_call(
        final_kernel,
        out_shape=struct(rows, width),
        grid_spec=pltpu.PrefetchScalarGridSpec(
            num_scalar_prefetch=1,
            grid=(rows // tile, pairs),
            in_specs=[
                pl.BlockSpec((tile, PAIR), lambda i, h, *_: (i, 3 * pairs + h)),
                pl.BlockSpec((count, PAIR), lambda i, h, *_: (0, h)),
                pl.BlockSpec((count, PAIR), lambda i, h, *_: (0, pairs + h)),
                spec,
                spec,
                full,
                whole(w_out),
                whole(w_cross_out),
            ],
            out_specs=full,
            scratch_shapes=[pltpu.VMEM((pairs, tile, PAIR), BF16)],
        ),
        compiler_params=params(WIDE),
        cost_estimate=cost(16 * rows * count * width, 28 * rows * width, 12 * rows * count),
    )(live, projected, anchor_kv, anchor_kv, *state, block_attn, w_out, w_cross_out)


def after(*arrays):
    return lax.optimization_barrier(arrays)


def permute(array, target):
    size = lax.axis_size("dom")
    pairs = [(i, target(i)) for i in range(size) if 0 <= target(i) < size]
    return lax.ppermute(array, "dom", pairs)


def local(
    points,
    norm_gain,
    w_qkv,
    w_out,
    w_cross_q,
    w_cross_kv,
    w_cross_out,
    live_blocks,
    send_blocks,
    neighbours,
    neighbour_count,
    anchor_index,
):
    rows, width = points.shape
    gain = norm_gain.reshape(1, width)
    size = lax.axis_size("dom")
    column, ring = 2, 4
    anchors, to_prev, to_next = pick(points, send_blocks, anchor_index)

    def around(array):
        return [permute(array, lambda i, n=n: (i + n * ring) % size) for n in (1, -1, 2)]

    beside = permute(anchors, lambda i: i ^ column)
    low = permute(to_next, lambda i: i + 1)
    high = permute(to_prev, lambda i: i - 1)
    rows_here = around(anchors)
    points, anchors = after(points, anchors)
    projected = project(points, gain, w_qkv, w_cross_q)
    beside, projected = after(beside, projected)
    rows_beside = around(beside)
    block_attn = block_attention(
        projected, low, high, gain, w_qkv, neighbours, neighbour_count, live_blocks
    )
    *parts, block_attn = after(anchors, beside, *rows_here, *rows_beside, block_attn)
    kv_own = anchor_project(parts, gain, w_cross_kv)
    kv_other = permute(kv_own, lambda i: i ^ 1)
    state = cross_part(projected, kv_own)
    return finish(projected, kv_other, state, block_attn, w_out, w_cross_out, live_blocks)


def solution(mesh):
    sharded = P(("car", "dom"))
    in_specs = (
        P(("car", "dom"), None),
        P(),
        P(),
        P(),
        P(),
        P(),
        P(),
        sharded,
        sharded,
        P(("car", "dom"), None),
        sharded,
        sharded,
    )
    out_specs = P(("car", "dom"), None)
    return jax.shard_map(local, mesh=mesh, in_specs=in_specs, out_specs=out_specs, check_vma=False)
```

```python
import functools

import jax
import jax.numpy as jnp
from jax import lax
from jax.experimental import pallas as pl
from jax.experimental.pallas import tpu as pltpu
from jax.sharding import PartitionSpec as P

HEADS = 12
BLK = 128
HB = 2
PAIR = 128
HALF = 64
CHUNK = 256
SCALE = HALF**-0.5 * 1.4426950408889634
LIMIT = 32 * 2**20
WIDE = 61 * 2**20
NEG = -1e30
F32 = jnp.float32
BF16 = jnp.bfloat16


def params(limit=LIMIT):
    return pltpu.CompilerParams(vmem_limit_bytes=limit)


def cost(flops, nbytes, trans=0):
    return pl.CostEstimate(flops=int(flops), bytes_accessed=int(nbytes), transcendentals=int(trans))


def struct(rows, cols, dtype=BF16):
    return jax.ShapeDtypeStruct((rows, cols), dtype)


def whole(array):
    return pl.BlockSpec(array.shape, lambda *_: (0,) * array.ndim)


def mm(a, b):
    return jnp.dot(a, b, preferred_element_type=F32)


def mm_t(a, b):
    return lax.dot_general(a, b, (((1,), (1,)), ((), ())), preferred_element_type=F32)


def normed_rows(rows, gain):
    floats = rows.astype(F32)
    factor = lax.rsqrt(jnp.mean(floats * floats, axis=-1, keepdims=True) + 1e-06)
    return (floats * factor * gain).astype(BF16)


def pick_kernel(send_ref, index_ref, source_ref, anchor_ref, prev_ref, next_ref, points_ref, sem):
    copy = pltpu.make_async_copy(source_ref, points_ref, sem)
    copy.start()
    rows = points_ref.shape[0]
    anchors = index_ref.shape[1]
    slot = lax.broadcasted_iota(jnp.int32, (rows, anchors), 0)
    chosen = jnp.where(slot == index_ref[...], 1.0, 0.0).astype(BF16)
    copy.wait()
    anchor_ref[...] = lax.dot_general(
        chosen, points_ref[...], (((0,), (0,)), ((), ())), preferred_element_type=F32
    ).astype(BF16)
    for place in range(HB):
        for base, out_ref in ((0, prev_ref), (HB, next_ref)):
            start = pl.multiple_of(send_ref[base + place] * BLK, BLK)
            out_ref[place * BLK : (place + 1) * BLK, :] = points_ref[pl.ds(start, BLK), :]


def pick(points, send_blocks, anchor_index):
    rows, width = points.shape
    anchors = anchor_index.shape[0]
    index = anchor_index.reshape(1, anchors)
    own = struct(anchors, width)
    side = struct(HB * BLK, width)
    return pl.pallas_call(
        pick_kernel,
        out_shape=(own, side, side),
        in_specs=[
            pl.BlockSpec(memory_space=pltpu.SMEM),
            pl.BlockSpec(memory_space=pltpu.VMEM),
            pl.BlockSpec(memory_space=pltpu.HBM),
        ],
        scratch_shapes=[pltpu.VMEM((rows, width), BF16), pltpu.SemaphoreType.DMA],
        compiler_params=params(WIDE),
        cost_estimate=cost(2 * anchors * rows * width, 4 * rows * width),
    )(send_blocks, index, points)


def project_kernel(points_ref, gain_ref, wqkv_ref, wcq_ref, out_ref, normed_ref):
    step = pl.program_id(0)
    rows = points_ref.shape[0]
    tile = rows // 4

    @pl.when(step == 0)
    def _():
        for at in range(0, rows, tile):
            normed = normed_rows(points_ref[at : at + tile, :], gain_ref[...])
            normed_ref[at : at + tile, :] = normed
            out_ref[at : at + tile, :] = (mm(normed, wqkv_ref[...]) * SCALE).astype(BF16)

    @pl.when((step == 1) | (step == 2))
    def _():
        out_ref[...] = mm(normed_ref[...], wqkv_ref[...]).astype(BF16)

    @pl.when(step == 3)
    def _():
        out_ref[...] = (mm(normed_ref[...], wcq_ref[...]) * SCALE).astype(BF16)


def project(points, gain, w_qkv, w_cross_q):
    rows, width = points.shape
    return pl.pallas_call(
        project_kernel,
        out_shape=struct(rows, 4 * width),
        grid=(4,),
        in_specs=[
            whole(points),
            whole(gain),
            pl.BlockSpec((width, width), lambda i: (0, jnp.minimum(i, 2))),
            whole(w_cross_q),
        ],
        out_specs=pl.BlockSpec((rows, width), lambda i: (0, i)),
        scratch_shapes=[pltpu.VMEM((rows, width), BF16)],
        compiler_params=params(),
        cost_estimate=cost(2 * rows * width * 4 * width, 20 * rows * width),
    )(points, gain, w_qkv, w_cross_q)


def split_heads(rows):
    lane = lax.broadcasted_iota(jnp.int32, rows.shape, 1)
    zero = jnp.zeros_like(rows)
    return jnp.concatenate(
        [jnp.where(lane < HALF, rows, zero), jnp.where(lane >= HALF, rows, zero)], axis=0
    )


def join_heads(both):
    count = both.shape[0] // 2
    lane = lax.broadcasted_iota(jnp.int32, (count, PAIR), 1)
    return jnp.where(lane < HALF, both[:count], both[count:])


def weigh(weights, values):
    ones = jnp.ones((values.shape[0], PAIR), BF16)
    return mm(weights.astype(BF16), jnp.concatenate([values, ones], axis=1))


def block_kernel(
    ids_ref,
    count_ref,
    live_ref,
    queries_ref,
    projected_ref,
    low_ref,
    high_ref,
    gain_ref,
    wk_ref,
    wv_ref,
    out_ref,
    table_ref,
    sems,
):
    block = pl.program_id(0)
    slots = ids_ref.shape[1]
    rows = projected_ref.shape[0]
    side, width = low_ref.shape

    @pl.when(block == 0)
    def _():
        copies = [
            pltpu.make_async_copy(
                projected_ref.at[:, (1 + n) * width : (2 + n) * width],
                table_ref.at[n, :rows],
                sems.at[n],
            )
            for n in range(2)
        ]
        for copy in copies:
            copy.start()
        for place, ref in enumerate((low_ref, high_ref)):
            normed = normed_rows(ref[...], gain_ref[...])
            at = rows + place * side
            table_ref[0, at : at + side, :] = mm(normed, wk_ref[...]).astype(BF16)
            table_ref[1, at : at + side, :] = mm(normed, wv_ref[...]).astype(BF16)
        for copy in copies:
            copy.wait()

    count = count_ref[block]
    pairs = jnp.where(block < live_ref[0], (count + 1) // 2, 0)

    @pl.when(pairs == 0)
    def _():
        out_ref[...] = jnp.zeros_like(out_ref)

    for used in range(1, slots // 2 + 1):

        @pl.when(pairs == used)
        def _(used=used):
            starts = [pl.multiple_of(ids_ref[block, n] * BLK, BLK) for n in range(2 * used)]
            dropped = jnp.where(count == 2 * used, 0.0, NEG)

            def rows_of(which, part, at):
                return jnp.concatenate(
                    [
                        table_ref[which, pl.ds(start, BLK), at : at + PAIR]
                        for start in starts[2 * part : 2 * part + 2]
                    ],
                    axis=0,
                )

            for at in range(0, width, PAIR):
                query = split_heads(queries_ref[:, at : at + PAIR])
                scores = [mm_t(query, rows_of(0, part, at)) for part in range(used)]
                last = scores[-1]
                scores[-1] = jnp.concatenate([last[:, :BLK], last[:, BLK:] + dropped], axis=1)
                top = functools.reduce(jnp.maximum, scores)
                top = jnp.max(top, axis=1, keepdims=True)
                total = sum(
                    weigh(jnp.exp2(scores[part] - top), rows_of(1, part, at))
                    for part in range(used)
                )
                out_ref[:, at : at + PAIR] = join_heads(total[:, :PAIR] / total[:, PAIR:]).astype(
                    BF16
                )


def block_attention(projected, low, high, gain, w_qkv, ids, counts, live):
    rows = projected.shape[0]
    width = low.shape[1]
    side = low.shape[0]
    blocks = rows // BLK
    return pl.pallas_call(
        block_kernel,
        out_shape=struct(rows, width),
        grid_spec=pltpu.PrefetchScalarGridSpec(
            num_scalar_prefetch=3,
            grid=(blocks,),
            in_specs=[
                pl.BlockSpec((BLK, width), lambda i, *_: (i, 0)),
                pl.BlockSpec(memory_space=pl.ANY),
                whole(low),
                whole(high),
                whole(gain),
                pl.BlockSpec((width, width), lambda i, *_: (0, 1)),
                pl.BlockSpec((width, width), lambda i, *_: (0, 2)),
            ],
            out_specs=pl.BlockSpec((BLK, width), lambda i, *_: (i, 0)),
            scratch_shapes=[
                pltpu.VMEM((2, rows + 2 * side, width), BF16),
                pltpu.SemaphoreType.DMA((2,)),
            ],
        ),
        compiler_params=params(),
        cost_estimate=cost(16 * rows * 5 * BLK * width, 12 * rows * width, rows * 5 * BLK * 12),
    )(ids, counts, live, projected, projected, low, high, gain, w_qkv, w_qkv)


def anchor_kernel(count, *refs):
    parts = refs[:count]
    gain_ref, weight_ref, out_ref, held_ref, sems = refs[count:]
    rows = parts[0].shape[0]
    normed = normed_rows(parts[0][...], gain_ref[...])
    stores = []
    for part in range(count):
        slot = part % 2
        if part >= 2:
            stores[part - 2].wait()
        held_ref[slot] = mm(normed, weight_ref[...]).astype(BF16)
        if part + 1 < count:
            normed = normed_rows(parts[part + 1][...], gain_ref[...])
        store = pltpu.make_async_copy(
            held_ref.at[slot], out_ref.at[part * rows : (part + 1) * rows], sems.at[slot]
        )
        store.start()
        stores.append(store)
    for store in stores[-2:]:
        store.wait()


def anchor_project(parts, gain, weight):
    rows, width = parts[0].shape
    every = len(parts) * rows
    vmem = pl.BlockSpec(memory_space=pltpu.VMEM)
    return pl.pallas_call(
        functools.partial(anchor_kernel, len(parts)),
        out_shape=struct(every, 2 * width),
        in_specs=[vmem] * (len(parts) + 2),
        out_specs=pl.BlockSpec(memory_space=pltpu.HBM),
        scratch_shapes=[
            pltpu.VMEM((2, rows, 2 * width), BF16),
            pltpu.SemaphoreType.DMA((2,)),
        ],
        compiler_params=params(),
        cost_estimate=cost(4 * every * width * width, 6 * every * width),
    )(*parts, gain, weight)


def sweep(query, keys_ref, values_ref):
    top, total = None, None
    for start in range(0, keys_ref.shape[0], CHUNK):
        scores = mm_t(query, keys_ref[start : start + CHUNK, :])
        values = values_ref[start : start + CHUNK, :]
        here = jnp.max(scores, axis=1, keepdims=True)
        if top is None:
            top = here
            total = weigh(jnp.exp2(scores - top), values)
        else:
            later = jnp.maximum(top, here)
            total = total * jnp.exp2(top - later) + weigh(jnp.exp2(scores - later), values)
            top = later
    sums = total[:, PAIR:]
    return join_heads(total[:, :PAIR] / sums), join_heads(top + jnp.log2(sums))


def cross_kernel(queries_ref, keys_ref, values_ref, mean_ref, size_ref):
    query = split_heads(queries_ref[...])
    mean_ref[...], size_ref[...] = sweep(query, keys_ref, values_ref)


def cross_part(projected, anchor_kv):
    rows = projected.shape[0]
    width = projected.shape[1] // 4
    count = anchor_kv.shape[0]
    pairs = width // PAIR
    tile = 512
    state = struct(rows, width, F32)
    spec = pl.BlockSpec((tile, PAIR), lambda h, i: (i, h))
    return pl.pallas_call(
        cross_kernel,
        out_shape=(state, state),
        grid=(pairs, rows // tile),
        in_specs=[
            pl.BlockSpec((tile, PAIR), lambda h, i: (i, 3 * pairs + h)),
            pl.BlockSpec((count, PAIR), lambda h, i: (0, h)),
            pl.BlockSpec((count, PAIR), lambda h, i: (0, pairs + h)),
        ],
        out_specs=[spec, spec],
        compiler_params=params(WIDE),
        cost_estimate=cost(16 * rows * count * width, 20 * rows * width, 12 * rows * count),
    )(projected, anchor_kv, anchor_kv)


def final_kernel(
    live_ref,
    queries_ref,
    keys_ref,
    values_ref,
    mean_ref,
    size_ref,
    block_ref,
    wout_ref,
    wcross_ref,
    out_ref,
    held_ref,
):
    pair = pl.program_id(1)
    rows = queries_ref.shape[0]
    query = split_heads(queries_ref[...])
    mean, size = sweep(query, keys_ref, values_ref)
    top = jnp.maximum(size, size_ref[...])
    share, other = jnp.exp2(size - top), jnp.exp2(size_ref[...] - top)
    held_ref[pair] = ((mean * share + mean_ref[...] * other) / (share + other)).astype(BF16)

    @pl.when(pair == pl.num_programs(1) - 1)
    def _():
        cross = jnp.concatenate([held_ref[n] for n in range(held_ref.shape[0])], axis=1)
        mixed = mm(block_ref[...], wout_ref[...]) + mm(cross, wcross_ref[...])
        place = lax.broadcasted_iota(jnp.int32, (rows, 1), 0) + pl.program_id(0) * rows
        out_ref[...] = jnp.where(place // BLK < live_ref[0], mixed, 0.0).astype(BF16)


def finish(projected, anchor_kv, state, block_attn, w_out, w_cross_out, live):
    rows = projected.shape[0]
    width = projected.shape[1] // 4
    count = anchor_kv.shape[0]
    pairs = width // PAIR
    tile = 512
    spec = pl.BlockSpec((tile, PAIR), lambda i, h, *_: (i, h))
    full = pl.BlockSpec((tile, width), lambda i, h, *_: (i, 0))
    return pl.pallas_call(
        final_kernel,
        out_shape=struct(rows, width),
        grid_spec=pltpu.PrefetchScalarGridSpec(
            num_scalar_prefetch=1,
            grid=(rows // tile, pairs),
            in_specs=[
                pl.BlockSpec((tile, PAIR), lambda i, h, *_: (i, 3 * pairs + h)),
                pl.BlockSpec((count, PAIR), lambda i, h, *_: (0, h)),
                pl.BlockSpec((count, PAIR), lambda i, h, *_: (0, pairs + h)),
                spec,
                spec,
                full,
                whole(w_out),
                whole(w_cross_out),
            ],
            out_specs=full,
            scratch_shapes=[pltpu.VMEM((pairs, tile, PAIR), BF16)],
        ),
        compiler_params=params(WIDE),
        cost_estimate=cost(16 * rows * count * width, 28 * rows * width, 12 * rows * count),
    )(live, projected, anchor_kv, anchor_kv, *state, block_attn, w_out, w_cross_out)


def after(*arrays):
    return lax.optimization_barrier(arrays)


def permute(array, target):
    size = lax.axis_size("dom")
    pairs = [(i, target(i)) for i in range(size) if 0 <= target(i) < size]
    return lax.ppermute(array, "dom", pairs)


def local(
    points,
    norm_gain,
    w_qkv,
    w_out,
    w_cross_q,
    w_cross_kv,
    w_cross_out,
    live_blocks,
    send_blocks,
    neighbours,
    neighbour_count,
    anchor_index,
):
    rows, width = points.shape
    gain = norm_gain.reshape(1, width)
    size = lax.axis_size("dom")
    column, ring = 2, 4
    anchors, to_prev, to_next = pick(points, send_blocks, anchor_index)

    def around(array):
        return [permute(array, lambda i, n=n: (i + n * ring) % size) for n in (1, -1, 2)]

    beside = permute(anchors, lambda i: i ^ column)
    low = permute(to_next, lambda i: i + 1)
    high = permute(to_prev, lambda i: i - 1)
    rows_here = around(anchors)
    points, anchors = after(points, anchors)
    projected = project(points, gain, w_qkv, w_cross_q)
    beside, rows_here[0], rows_here[1], projected = after(
        beside, rows_here[0], rows_here[1], projected
    )
    rows_beside = [permute(rows_here[n], lambda i: i ^ column) for n in range(2)]
    rows_beside.append(permute(beside, lambda i: (i + 2 * ring) % size))
    block_attn = block_attention(
        projected, low, high, gain, w_qkv, neighbours, neighbour_count, live_blocks
    )
    *parts, block_attn = after(anchors, beside, *rows_here, *rows_beside, block_attn)
    kv_own = anchor_project(parts, gain, w_cross_kv)
    kv_other = permute(kv_own, lambda i: i ^ 1)
    state = cross_part(projected, kv_own)
    return finish(projected, kv_other, state, block_attn, w_out, w_cross_out, live_blocks)


def solution(mesh):
    sharded = P(("car", "dom"))
    in_specs = (
        P(("car", "dom"), None),
        P(),
        P(),
        P(),
        P(),
        P(),
        P(),
        sharded,
        sharded,
        P(("car", "dom"), None),
        sharded,
        sharded,
    )
    out_specs = P(("car", "dom"), None)
    return jax.shard_map(local, mesh=mesh, in_specs=in_specs, out_specs=out_specs, check_vma=False)
```

```python
import functools

import jax
import jax.numpy as jnp
from jax import lax
from jax.experimental import pallas as pl
from jax.experimental.pallas import tpu as pltpu
from jax.sharding import PartitionSpec as P

HEADS = 12
BLK = 128
HB = 2
PAIR = 128
HALF = 64
CHUNK = 512
SCALE = HALF**-0.5 * 1.4426950408889634
LIMIT = 32 * 2**20
WIDE = 61 * 2**20
NEG = -1e30
F32 = jnp.float32
BF16 = jnp.bfloat16


def params(limit=LIMIT):
    return pltpu.CompilerParams(vmem_limit_bytes=limit)


def cost(flops, nbytes, trans=0):
    return pl.CostEstimate(flops=int(flops), bytes_accessed=int(nbytes), transcendentals=int(trans))


def struct(rows, cols, dtype=BF16):
    return jax.ShapeDtypeStruct((rows, cols), dtype)


def whole(array):
    return pl.BlockSpec(array.shape, lambda *_: (0,) * array.ndim)


def mm(a, b):
    return jnp.dot(a, b, preferred_element_type=F32)


def mm_t(a, b):
    return lax.dot_general(a, b, (((1,), (1,)), ((), ())), preferred_element_type=F32)


def normed_rows(rows, gain):
    floats = rows.astype(F32)
    factor = lax.rsqrt(jnp.mean(floats * floats, axis=-1, keepdims=True) + 1e-06)
    return (floats * factor * gain).astype(BF16)


def pick_kernel(send_ref, index_ref, source_ref, anchor_ref, prev_ref, next_ref, points_ref, sem):
    copy = pltpu.make_async_copy(source_ref, points_ref, sem)
    copy.start()
    rows = points_ref.shape[0]
    anchors = index_ref.shape[1]
    slot = lax.broadcasted_iota(jnp.int32, (rows, anchors), 0)
    chosen = jnp.where(slot == index_ref[...], 1.0, 0.0).astype(BF16)
    copy.wait()
    anchor_ref[...] = lax.dot_general(
        chosen, points_ref[...], (((0,), (0,)), ((), ())), preferred_element_type=F32
    ).astype(BF16)
    for place in range(HB):
        for base, out_ref in ((0, prev_ref), (HB, next_ref)):
            start = pl.multiple_of(send_ref[base + place] * BLK, BLK)
            out_ref[place * BLK : (place + 1) * BLK, :] = points_ref[pl.ds(start, BLK), :]


def pick(points, send_blocks, anchor_index):
    rows, width = points.shape
    anchors = anchor_index.shape[0]
    index = anchor_index.reshape(1, anchors)
    own = struct(anchors, width)
    side = struct(HB * BLK, width)
    return pl.pallas_call(
        pick_kernel,
        out_shape=(own, side, side),
        in_specs=[
            pl.BlockSpec(memory_space=pltpu.SMEM),
            pl.BlockSpec(memory_space=pltpu.VMEM),
            pl.BlockSpec(memory_space=pltpu.HBM),
        ],
        scratch_shapes=[pltpu.VMEM((rows, width), BF16), pltpu.SemaphoreType.DMA],
        compiler_params=params(WIDE),
        cost_estimate=cost(2 * anchors * rows * width, 4 * rows * width),
    )(send_blocks, index, points)


def project_kernel(points_ref, gain_ref, wqkv_ref, wcq_ref, out_ref, normed_ref):
    step = pl.program_id(0)
    rows = points_ref.shape[0]
    tile = rows // 4

    @pl.when(step == 0)
    def _():
        for at in range(0, rows, tile):
            normed = normed_rows(points_ref[at : at + tile, :], gain_ref[...])
            normed_ref[at : at + tile, :] = normed
            out_ref[at : at + tile, :] = (mm(normed, wqkv_ref[...]) * SCALE).astype(BF16)

    @pl.when((step == 1) | (step == 2))
    def _():
        out_ref[...] = mm(normed_ref[...], wqkv_ref[...]).astype(BF16)

    @pl.when(step == 3)
    def _():
        out_ref[...] = (mm(normed_ref[...], wcq_ref[...]) * SCALE).astype(BF16)


def project(points, gain, w_qkv, w_cross_q):
    rows, width = points.shape
    return pl.pallas_call(
        project_kernel,
        out_shape=struct(rows, 4 * width),
        grid=(4,),
        in_specs=[
            whole(points),
            whole(gain),
            pl.BlockSpec((width, width), lambda i: (0, jnp.minimum(i, 2))),
            whole(w_cross_q),
        ],
        out_specs=pl.BlockSpec((rows, width), lambda i: (0, i)),
        scratch_shapes=[pltpu.VMEM((rows, width), BF16)],
        compiler_params=params(),
        cost_estimate=cost(2 * rows * width * 4 * width, 20 * rows * width),
    )(points, gain, w_qkv, w_cross_q)


def split_heads(rows):
    lane = lax.broadcasted_iota(jnp.int32, rows.shape, 1)
    zero = jnp.zeros_like(rows)
    return jnp.concatenate(
        [jnp.where(lane < HALF, rows, zero), jnp.where(lane >= HALF, rows, zero)], axis=0
    )


def join_heads(both):
    count = both.shape[0] // 2
    lane = lax.broadcasted_iota(jnp.int32, (count, PAIR), 1)
    return jnp.where(lane < HALF, both[:count], both[count:])


def weigh(weights, values):
    weights = weights.astype(BF16)
    count = weights.shape[0] // 2
    lane = lax.broadcasted_iota(jnp.int32, values.shape, 1)
    one = jnp.ones_like(values)
    return jnp.concatenate(
        [
            mm(weights[:count], jnp.where(lane < HALF, values, one)),
            mm(weights[count:], jnp.where(lane < HALF, one, values)),
        ],
        axis=0,
    )


def weigh_wide(weights, values):
    ones = jnp.ones((values.shape[0], PAIR), BF16)
    return mm(weights.astype(BF16), jnp.concatenate([values, ones], axis=1))


def block_kernel(
    ids_ref,
    count_ref,
    live_ref,
    projected_ref,
    low_ref,
    high_ref,
    gain_ref,
    weight_ref,
    out_ref,
    table_ref,
):
    block = pl.program_id(0)
    slots = ids_ref.shape[1]
    blocks = count_ref.shape[0]
    width = low_ref.shape[1]

    @pl.when(block == 0)
    def _():
        rows = jnp.concatenate([low_ref[...], high_ref[...]], axis=0)
        normed = normed_rows(rows, gain_ref[...])
        for n in range(2):
            table_ref[n] = mm(normed, weight_ref[:, (1 + n) * width : (2 + n) * width]).astype(BF16)

    count = count_ref[block]
    pairs = jnp.where(block < live_ref[0], (count + 1) // 2, 0)

    @pl.when(pairs == 0)
    def _():
        out_ref[...] = jnp.zeros_like(out_ref)

    for used in range(1, slots // 2 + 1):

        @pl.when(pairs == used)
        def _(used=used):
            places = []
            for n in range(2 * used):
                place = ids_ref[block, n]
                own = pl.multiple_of(jnp.minimum(place, blocks - 1) * BLK, BLK)
                received = pl.multiple_of(jnp.maximum(place - blocks, 0) * BLK, BLK)
                places.append((place < blocks, own, received))
            dropped = jnp.where(count == 2 * used, 0.0, NEG)
            here = pl.ds(pl.multiple_of(block * BLK, BLK), BLK)

            def rows_of(which, part, at):
                lanes = slice((1 + which) * width + at, (1 + which) * width + at + PAIR)
                return jnp.concatenate(
                    [
                        jnp.where(
                            is_own,
                            projected_ref[pl.ds(own, BLK), lanes],
                            table_ref[which, pl.ds(received, BLK), at : at + PAIR],
                        )
                        for is_own, own, received in places[2 * part : 2 * part + 2]
                    ],
                    axis=0,
                )

            for at in range(0, width, PAIR):
                query = split_heads(projected_ref[here, at : at + PAIR])
                scores = [mm_t(query, rows_of(0, part, at)) for part in range(used)]
                last = scores[-1]
                scores[-1] = jnp.concatenate([last[:, :BLK], last[:, BLK:] + dropped], axis=1)
                top = functools.reduce(jnp.maximum, scores)
                top = jnp.max(top, axis=1, keepdims=True)
                total = sum(
                    weigh_wide(jnp.exp2(scores[part] - top), rows_of(1, part, at))
                    for part in range(used)
                )
                out_ref[:, at : at + PAIR] = join_heads(total[:, :PAIR] / total[:, PAIR:]).astype(
                    BF16
                )


def block_attention(projected, low, high, gain, w_qkv, ids, counts, live):
    rows = projected.shape[0]
    width = low.shape[1]
    side = low.shape[0]
    blocks = rows // BLK
    vmem = pl.BlockSpec(memory_space=pltpu.VMEM)
    return pl.pallas_call(
        block_kernel,
        out_shape=struct(rows, width),
        grid_spec=pltpu.PrefetchScalarGridSpec(
            num_scalar_prefetch=3,
            grid=(blocks,),
            in_specs=[vmem, vmem, vmem, vmem, vmem],
            out_specs=pl.BlockSpec((BLK, width), lambda i, *_: (i, 0)),
            scratch_shapes=[pltpu.VMEM((2, 2 * side, width), BF16)],
        ),
        compiler_params=params(),
        cost_estimate=cost(16 * rows * 5 * BLK * width, 12 * rows * width, rows * 5 * BLK * 12),
    )(ids, counts, live, projected, low, high, gain, w_qkv)


def anchor_kernel(count, *refs):
    parts = refs[:count]
    gain_ref, weight_ref, out_ref, normed_ref, held_ref, sems = refs[count:]
    rows, width = parts[0].shape
    group = normed_ref.shape[0] // rows
    stores = []
    for first in range(0, count, group):
        for part in range(group):
            normed_ref[part * rows : (part + 1) * rows, :] = normed_rows(
                parts[first + part][...], gain_ref[...]
            )
        for n in range(2):
            slot = len(stores) % 2
            if len(stores) >= 2:
                stores[-2].wait()
            columns = slice(n * width, (n + 1) * width)
            held_ref[slot] = mm(normed_ref[...], weight_ref[:, columns]).astype(BF16)
            store = pltpu.make_async_copy(
                held_ref.at[slot],
                out_ref.at[first * rows : (first + group) * rows, columns],
                sems.at[slot],
            )
            store.start()
            stores.append(store)
    for store in stores[-2:]:
        store.wait()


def anchor_project(parts, gain, weight):
    rows, width = parts[0].shape
    every = len(parts) * rows
    vmem = pl.BlockSpec(memory_space=pltpu.VMEM)
    group = len(parts) // 2 * rows
    return pl.pallas_call(
        functools.partial(anchor_kernel, len(parts)),
        out_shape=struct(every, 2 * width),
        in_specs=[vmem] * (len(parts) + 2),
        out_specs=pl.BlockSpec(memory_space=pltpu.HBM),
        scratch_shapes=[
            pltpu.VMEM((group, width), BF16),
            pltpu.VMEM((2, group, width), BF16),
            pltpu.SemaphoreType.DMA((2,)),
        ],
        compiler_params=params(),
        cost_estimate=cost(4 * every * width * width, 6 * every * width),
    )(*parts, gain, weight)


def sweep(query, keys_ref, values_ref):
    top, total = None, None
    for start in range(0, keys_ref.shape[0], CHUNK):
        scores = mm_t(query, keys_ref[start : start + CHUNK, :])
        values = values_ref[start : start + CHUNK, :]
        here = jnp.max(scores, axis=1, keepdims=True)
        if top is None:
            top = here
            total = weigh(jnp.exp2(scores - top), values)
        else:
            later = jnp.maximum(top, here)
            total = total * jnp.exp2(top - later) + weigh(jnp.exp2(scores - later), values)
            top = later
    sums = pltpu.roll(total, HALF, 1)
    return join_heads(total / sums), join_heads(top + jnp.log2(sums))


def cross_kernel(queries_ref, keys_ref, values_ref, mean_ref, size_ref):
    query = split_heads(queries_ref[...])
    mean_ref[...], size_ref[...] = sweep(query, keys_ref, values_ref)


def cross_part(projected, anchor_kv):
    rows = projected.shape[0]
    width = projected.shape[1] // 4
    count = anchor_kv.shape[0]
    pairs = width // PAIR
    tile = rows
    state = struct(rows, width, F32)
    spec = pl.BlockSpec((tile, PAIR), lambda h, i: (i, h))
    return pl.pallas_call(
        cross_kernel,
        out_shape=(state, state),
        grid=(pairs, rows // tile),
        in_specs=[
            pl.BlockSpec((tile, PAIR), lambda h, i: (i, 3 * pairs + h)),
            pl.BlockSpec((count, PAIR), lambda h, i: (0, h)),
            pl.BlockSpec((count, PAIR), lambda h, i: (0, pairs + h)),
        ],
        out_specs=[spec, spec],
        compiler_params=params(WIDE),
        cost_estimate=cost(16 * rows * count * width, 20 * rows * width, 12 * rows * count),
    )(projected, anchor_kv, anchor_kv)


def final_kernel(
    live_ref,
    queries_ref,
    keys_ref,
    values_ref,
    mean_ref,
    size_ref,
    block_source_ref,
    wout_source_ref,
    wcross_source_ref,
    out_ref,
    held_ref,
    block_ref,
    wout_ref,
    wcross_ref,
    sems,
):
    pair = pl.program_id(0)
    rows = queries_ref.shape[0]
    fetches = [
        pltpu.make_async_copy(source, target, sems.at[n])
        for n, (source, target) in enumerate(
            [
                (block_source_ref, block_ref),
                (wout_source_ref, wout_ref),
                (wcross_source_ref, wcross_ref),
            ]
        )
    ]

    @pl.when(pair == 0)
    def _():
        for fetch in fetches:
            fetch.start()

    query = split_heads(queries_ref[...])
    mean, size = sweep(query, keys_ref, values_ref)
    top = jnp.maximum(size, size_ref[...])
    share, other = jnp.exp2(size - top), jnp.exp2(size_ref[...] - top)
    held_ref[pair] = ((mean * share + mean_ref[...] * other) / (share + other)).astype(BF16)

    @pl.when(pair == pl.num_programs(0) - 1)
    def _():
        for fetch in fetches:
            fetch.wait()
        cross = jnp.concatenate([held_ref[n] for n in range(held_ref.shape[0])], axis=1)
        mixed = mm(block_ref[...], wout_ref[...]) + mm(cross, wcross_ref[...])
        place = lax.broadcasted_iota(jnp.int32, (rows, 1), 0)
        out_ref[...] = jnp.where(place // BLK < live_ref[0], mixed, 0.0).astype(BF16)


def finish(projected, anchor_kv, state, block_attn, w_out, w_cross_out, live):
    rows = projected.shape[0]
    width = projected.shape[1] // 4
    count = anchor_kv.shape[0]
    pairs = width // PAIR
    spec = pl.BlockSpec((rows, PAIR), lambda h, *_: (0, h))
    hbm = pl.BlockSpec(memory_space=pltpu.HBM)
    return pl.pallas_call(
        final_kernel,
        out_shape=struct(rows, width),
        grid_spec=pltpu.PrefetchScalarGridSpec(
            num_scalar_prefetch=1,
            grid=(pairs,),
            in_specs=[
                pl.BlockSpec((rows, PAIR), lambda h, *_: (0, 3 * pairs + h)),
                pl.BlockSpec((count, PAIR), lambda h, *_: (0, h)),
                pl.BlockSpec((count, PAIR), lambda h, *_: (0, pairs + h)),
                spec,
                spec,
                hbm,
                hbm,
                hbm,
            ],
            out_specs=pl.BlockSpec((rows, width), lambda h, *_: (0, 0)),
            scratch_shapes=[
                pltpu.VMEM((pairs, rows, PAIR), BF16),
                pltpu.VMEM((rows, width), BF16),
                pltpu.VMEM((width, width), BF16),
                pltpu.VMEM((width, width), BF16),
                pltpu.SemaphoreType.DMA((3,)),
            ],
        ),
        compiler_params=params(WIDE),
        cost_estimate=cost(16 * rows * count * width, 28 * rows * width, 12 * rows * count),
    )(live, projected, anchor_kv, anchor_kv, *state, block_attn, w_out, w_cross_out)


def after(*arrays):
    return lax.optimization_barrier(arrays)


def permute(array, target):
    size = lax.axis_size("dom")
    pairs = [(i, target(i)) for i in range(size) if 0 <= target(i) < size]
    return lax.ppermute(array, "dom", pairs)


def local(
    points,
    norm_gain,
    w_qkv,
    w_out,
    w_cross_q,
    w_cross_kv,
    w_cross_out,
    live_blocks,
    send_blocks,
    neighbours,
    neighbour_count,
    anchor_index,
):
    rows, width = points.shape
    gain = norm_gain.reshape(1, width)
    size = lax.axis_size("dom")
    column, ring = 2, 4
    anchors, to_prev, to_next = pick(points, send_blocks, anchor_index)

    def around(array):
        return [permute(array, lambda i, n=n: (i + n * ring) % size) for n in (1, -1, 2)]

    beside = permute(anchors, lambda i: i ^ column)
    low = permute(to_next, lambda i: i + 1)
    high = permute(to_prev, lambda i: i - 1)
    rows_here = around(anchors)
    points, anchors = after(points, anchors)
    projected = project(points, gain, w_qkv, w_cross_q)
    beside, rows_here[0], rows_here[1], projected = after(
        beside, rows_here[0], rows_here[1], projected
    )
    rows_beside = [permute(rows_here[n], lambda i: i ^ column) for n in range(2)]
    rows_beside.append(permute(beside, lambda i: (i + 2 * ring) % size))
    block_attn = block_attention(
        projected, low, high, gain, w_qkv, neighbours, neighbour_count, live_blocks
    )
    *parts, block_attn = after(anchors, beside, *rows_here, *rows_beside, block_attn)
    kv_own = anchor_project(parts, gain, w_cross_kv)
    kv_other = permute(kv_own, lambda i: i ^ 1)
    state = cross_part(projected, kv_own)
    return finish(projected, kv_other, state, block_attn, w_out, w_cross_out, live_blocks)


def solution(mesh):
    sharded = P(("car", "dom"))
    in_specs = (
        P(("car", "dom"), None),
        P(),
        P(),
        P(),
        P(),
        P(),
        P(),
        sharded,
        sharded,
        P(("car", "dom"), None),
        sharded,
        sharded,
    )
    out_specs = P(("car", "dom"), None)
    return jax.shard_map(local, mesh=mesh, in_specs=in_specs, out_specs=out_specs, check_vma=False)
```

```python
import functools

import jax
import jax.numpy as jnp
from jax import lax
from jax.experimental import pallas as pl
from jax.experimental.pallas import tpu as pltpu
from jax.sharding import PartitionSpec as P

HEADS = 12
BLK = 128
HB = 2
PAIR = 128
HALF = 64
CHUNK = 512
SCALE = HALF**-0.5 * 1.4426950408889634
LIMIT = 32 * 2**20
WIDE = 61 * 2**20
NEG = -1e30
F32 = jnp.float32
BF16 = jnp.bfloat16


def params(limit=LIMIT):
    return pltpu.CompilerParams(vmem_limit_bytes=limit)


def cost(flops, nbytes, trans=0):
    return pl.CostEstimate(flops=int(flops), bytes_accessed=int(nbytes), transcendentals=int(trans))


def struct(rows, cols, dtype=BF16):
    return jax.ShapeDtypeStruct((rows, cols), dtype)


def whole(array):
    return pl.BlockSpec(array.shape, lambda *_: (0,) * array.ndim)


def mm(a, b):
    return jnp.dot(a, b, preferred_element_type=F32)


def mm_t(a, b):
    return lax.dot_general(a, b, (((1,), (1,)), ((), ())), preferred_element_type=F32)


def normed_rows(rows, gain):
    floats = rows.astype(F32)
    factor = lax.rsqrt(jnp.mean(floats * floats, axis=-1, keepdims=True) + 1e-06)
    return (floats * factor * gain).astype(BF16)


def pick_kernel(
    send_ref, index_ref, gain_ref, source_ref, anchor_ref, prev_ref, next_ref, points_ref, sem
):
    copy = pltpu.make_async_copy(source_ref, points_ref, sem)
    copy.start()
    rows = points_ref.shape[0]
    anchors = index_ref.shape[1]
    slot = lax.broadcasted_iota(jnp.int32, (rows, anchors), 0)
    chosen = jnp.where(slot == index_ref[...], 1.0, 0.0).astype(BF16)
    copy.wait()
    picked = lax.dot_general(
        chosen, points_ref[...], (((0,), (0,)), ((), ())), preferred_element_type=F32
    )
    anchor_ref[...] = normed_rows(picked, gain_ref[...])
    for place in range(HB):
        for base, out_ref in ((0, prev_ref), (HB, next_ref)):
            start = pl.multiple_of(send_ref[base + place] * BLK, BLK)
            out_ref[place * BLK : (place + 1) * BLK, :] = normed_rows(
                points_ref[pl.ds(start, BLK), :], gain_ref[...]
            )


def pick(points, gain, send_blocks, anchor_index):
    rows, width = points.shape
    anchors = anchor_index.shape[0]
    index = anchor_index.reshape(1, anchors)
    own = struct(anchors, width)
    side = struct(HB * BLK, width)
    vmem = pl.BlockSpec(memory_space=pltpu.VMEM)
    return pl.pallas_call(
        pick_kernel,
        out_shape=(own, side, side),
        in_specs=[
            pl.BlockSpec(memory_space=pltpu.SMEM),
            vmem,
            vmem,
            pl.BlockSpec(memory_space=pltpu.HBM),
        ],
        scratch_shapes=[pltpu.VMEM((rows, width), BF16), pltpu.SemaphoreType.DMA],
        compiler_params=params(WIDE),
        cost_estimate=cost(2 * anchors * rows * width, 4 * rows * width),
    )(send_blocks, index, gain, points)


def project_kernel(points_ref, gain_ref, wqkv_ref, wcq_ref, out_ref, normed_ref):
    rows, width = points_ref.shape
    tile = rows // 4
    for at in range(0, rows, tile):
        normed = normed_rows(points_ref[at : at + tile, :], gain_ref[...])
        normed_ref[at : at + tile, :] = normed
        out_ref[at : at + tile, :width] = (mm(normed, wqkv_ref[:, :width]) * SCALE).astype(BF16)
    for at in range(width, 3 * width, width):
        out_ref[:, at : at + width] = mm(normed_ref[...], wqkv_ref[:, at : at + width]).astype(BF16)
    out_ref[:, 3 * width :] = (mm(normed_ref[...], wcq_ref[...]) * SCALE).astype(BF16)


def project(points, gain, w_qkv, w_cross_q):
    rows, width = points.shape
    vmem = pl.BlockSpec(memory_space=pltpu.VMEM)
    return pl.pallas_call(
        project_kernel,
        out_shape=struct(rows, 4 * width),
        in_specs=[vmem] * 4,
        out_specs=vmem,
        scratch_shapes=[pltpu.VMEM((rows, width), BF16)],
        compiler_params=params(24 * 2**20),
        cost_estimate=cost(2 * rows * width * 4 * width, 20 * rows * width),
    )(points, gain, w_qkv, w_cross_q)


def split_heads(rows):
    lane = lax.broadcasted_iota(jnp.int32, rows.shape, 1)
    zero = jnp.zeros_like(rows)
    return jnp.concatenate(
        [jnp.where(lane < HALF, rows, zero), jnp.where(lane >= HALF, rows, zero)], axis=0
    )


def join_heads(both):
    count = both.shape[0] // 2
    lane = lax.broadcasted_iota(jnp.int32, (count, PAIR), 1)
    return jnp.where(lane < HALF, both[:count], both[count:])


def weigh(weights, values):
    weights = weights.astype(BF16)
    count = weights.shape[0] // 2
    lane = lax.broadcasted_iota(jnp.int32, values.shape, 1)
    one = jnp.ones_like(values)
    return jnp.concatenate(
        [
            mm(weights[:count], jnp.where(lane < HALF, values, one)),
            mm(weights[count:], jnp.where(lane < HALF, one, values)),
        ],
        axis=0,
    )


def weigh_wide(weights, values):
    ones = jnp.ones((values.shape[0], PAIR), BF16)
    return mm(weights.astype(BF16), jnp.concatenate([values, ones], axis=1))


def block_kernel(
    ids_ref,
    count_ref,
    live_ref,
    projected_ref,
    low_ref,
    high_ref,
    weight_ref,
    out_ref,
    table_ref,
):
    block = pl.program_id(0)
    slots = ids_ref.shape[1]
    blocks = count_ref.shape[0]
    width = low_ref.shape[1]

    @pl.when(block == 0)
    def _():
        normed = jnp.concatenate([low_ref[...], high_ref[...]], axis=0)
        for n in range(2):
            table_ref[n] = mm(normed, weight_ref[:, (1 + n) * width : (2 + n) * width]).astype(BF16)

    count = count_ref[block]
    pairs = jnp.where(block < live_ref[0], (count + 1) // 2, 0)

    @pl.when(pairs == 0)
    def _():
        out_ref[...] = jnp.zeros_like(out_ref)

    for used in range(1, slots // 2 + 1):

        @pl.when(pairs == used)
        def _(used=used):
            places = []
            for n in range(2 * used):
                place = ids_ref[block, n]
                own = pl.multiple_of(jnp.minimum(place, blocks - 1) * BLK, BLK)
                received = pl.multiple_of(jnp.maximum(place - blocks, 0) * BLK, BLK)
                places.append((place < blocks, own, received))
            dropped = jnp.where(count == 2 * used, 0.0, NEG)
            here = pl.ds(pl.multiple_of(block * BLK, BLK), BLK)

            def rows_of(which, part, at):
                lanes = slice((1 + which) * width + at, (1 + which) * width + at + PAIR)
                return jnp.concatenate(
                    [
                        jnp.where(
                            is_own,
                            projected_ref[pl.ds(own, BLK), lanes],
                            table_ref[which, pl.ds(received, BLK), at : at + PAIR],
                        )
                        for is_own, own, received in places[2 * part : 2 * part + 2]
                    ],
                    axis=0,
                )

            for at in range(0, width, PAIR):
                query = split_heads(projected_ref[here, at : at + PAIR])
                scores = [mm_t(query, rows_of(0, part, at)) for part in range(used)]
                last = scores[-1]
                scores[-1] = jnp.concatenate([last[:, :BLK], last[:, BLK:] + dropped], axis=1)
                top = functools.reduce(jnp.maximum, scores)
                top = jnp.max(top, axis=1, keepdims=True)
                total = sum(
                    weigh_wide(jnp.exp2(scores[part] - top), rows_of(1, part, at))
                    for part in range(used)
                )
                out_ref[:, at : at + PAIR] = join_heads(total[:, :PAIR] / total[:, PAIR:]).astype(
                    BF16
                )


def block_attention(projected, low, high, w_qkv, ids, counts, live):
    rows = projected.shape[0]
    width = low.shape[1]
    side = low.shape[0]
    blocks = rows // BLK
    vmem = pl.BlockSpec(memory_space=pltpu.VMEM)
    return pl.pallas_call(
        block_kernel,
        out_shape=struct(rows, width),
        grid_spec=pltpu.PrefetchScalarGridSpec(
            num_scalar_prefetch=3,
            grid=(blocks,),
            in_specs=[vmem] * 4,
            out_specs=pl.BlockSpec((BLK, width), lambda i, *_: (i, 0)),
            scratch_shapes=[pltpu.VMEM((2, 2 * side, width), BF16)],
        ),
        compiler_params=params(),
        cost_estimate=cost(16 * rows * 5 * BLK * width, 12 * rows * width, rows * 5 * BLK * 12),
    )(ids, counts, live, projected, low, high, w_qkv)


def anchor_kernel(count, *refs):
    parts = refs[:count]
    weight_ref, out_ref, held_ref, sems = refs[count:]
    rows, width = parts[0].shape
    group = count // 2
    stores = []
    for first in range(0, count, group):
        normed = jnp.concatenate([part[...] for part in parts[first : first + group]], axis=0)
        for n in range(2):
            columns = slice(n * width, (n + 1) * width)
            slot = len(stores)
            held_ref[slot] = mm(normed, weight_ref[:, columns]).astype(BF16)
            store = pltpu.make_async_copy(
                held_ref.at[slot],
                out_ref.at[first * rows : (first + group) * rows, columns],
                sems.at[slot],
            )
            store.start()
            stores.append(store)
    for store in stores:
        store.wait()


def anchor_project(parts, weight):
    rows, width = parts[0].shape
    every = len(parts) * rows
    vmem = pl.BlockSpec(memory_space=pltpu.VMEM)
    return pl.pallas_call(
        functools.partial(anchor_kernel, len(parts)),
        out_shape=struct(every, 2 * width),
        in_specs=[vmem] * (len(parts) + 1),
        out_specs=pl.BlockSpec(memory_space=pltpu.HBM),
        scratch_shapes=[
            pltpu.VMEM((4, every // 2, width), BF16),
            pltpu.SemaphoreType.DMA((4,)),
        ],
        compiler_params=params(),
        cost_estimate=cost(4 * every * width * width, 6 * every * width),
    )(*parts, weight)


def sweep(query, keys_ref, values_ref):
    top, total = None, None
    for start in range(0, keys_ref.shape[0], CHUNK):
        scores = mm_t(query, keys_ref[start : start + CHUNK, :])
        values = values_ref[start : start + CHUNK, :]
        here = jnp.max(scores, axis=1, keepdims=True)
        if top is None:
            top = here
            total = weigh(jnp.exp2(scores - top), values)
        else:
            later = jnp.maximum(top, here)
            total = total * jnp.exp2(top - later) + weigh(jnp.exp2(scores - later), values)
            top = later
    sums = pltpu.roll(total, HALF, 1)
    return join_heads(total / sums), join_heads(top + jnp.log2(sums))


def cross_kernel(queries_ref, keys_ref, values_ref, mean_ref, size_ref):
    query = split_heads(queries_ref[...])
    mean_ref[...], size_ref[...] = sweep(query, keys_ref, values_ref)


def cross_part(projected, anchor_kv):
    rows = projected.shape[0]
    width = projected.shape[1] // 4
    count = anchor_kv.shape[0]
    pairs = width // PAIR
    tile = rows
    state = struct(rows, width, F32)
    spec = pl.BlockSpec((tile, PAIR), lambda h, i: (i, h))
    return pl.pallas_call(
        cross_kernel,
        out_shape=(state, state),
        grid=(pairs, rows // tile),
        in_specs=[
            pl.BlockSpec((tile, PAIR), lambda h, i: (i, 3 * pairs + h)),
            pl.BlockSpec((count, PAIR), lambda h, i: (0, h)),
            pl.BlockSpec((count, PAIR), lambda h, i: (0, pairs + h)),
        ],
        out_specs=[spec, spec],
        compiler_params=params(WIDE),
        cost_estimate=cost(16 * rows * count * width, 20 * rows * width, 12 * rows * count),
    )(projected, anchor_kv, anchor_kv)


def final_kernel(
    live_ref,
    queries_ref,
    keys_ref,
    values_ref,
    mean_ref,
    size_ref,
    block_source_ref,
    wout_source_ref,
    wcross_source_ref,
    out_ref,
    held_ref,
    block_ref,
    wout_ref,
    wcross_ref,
    sems,
):
    pair = pl.program_id(0)
    rows = queries_ref.shape[0]
    fetches = [
        pltpu.make_async_copy(source, target, sems.at[n])
        for n, (source, target) in enumerate(
            [
                (block_source_ref, block_ref),
                (wout_source_ref, wout_ref),
                (wcross_source_ref, wcross_ref),
            ]
        )
    ]

    @pl.when(pair == 0)
    def _():
        for fetch in fetches:
            fetch.start()

    query = split_heads(queries_ref[...])
    mean, size = sweep(query, keys_ref, values_ref)
    top = jnp.maximum(size, size_ref[...])
    share, other = jnp.exp2(size - top), jnp.exp2(size_ref[...] - top)
    held_ref[pair] = ((mean * share + mean_ref[...] * other) / (share + other)).astype(BF16)

    @pl.when(pair == pl.num_programs(0) - 1)
    def _():
        for fetch in fetches:
            fetch.wait()
        cross = jnp.concatenate([held_ref[n] for n in range(held_ref.shape[0])], axis=1)
        mixed = mm(block_ref[...], wout_ref[...]) + mm(cross, wcross_ref[...])
        place = lax.broadcasted_iota(jnp.int32, (rows, 1), 0)
        out_ref[...] = jnp.where(place // BLK < live_ref[0], mixed, 0.0).astype(BF16)


def finish(projected, anchor_kv, state, block_attn, w_out, w_cross_out, live):
    rows = projected.shape[0]
    width = projected.shape[1] // 4
    count = anchor_kv.shape[0]
    pairs = width // PAIR
    spec = pl.BlockSpec((rows, PAIR), lambda h, *_: (0, h))
    hbm = pl.BlockSpec(memory_space=pltpu.HBM)
    return pl.pallas_call(
        final_kernel,
        out_shape=struct(rows, width),
        grid_spec=pltpu.PrefetchScalarGridSpec(
            num_scalar_prefetch=1,
            grid=(pairs,),
            in_specs=[
                pl.BlockSpec((rows, PAIR), lambda h, *_: (0, 3 * pairs + h)),
                pl.BlockSpec((count, PAIR), lambda h, *_: (0, h)),
                pl.BlockSpec((count, PAIR), lambda h, *_: (0, pairs + h)),
                spec,
                spec,
                hbm,
                hbm,
                hbm,
            ],
            out_specs=pl.BlockSpec((rows, width), lambda h, *_: (0, 0)),
            scratch_shapes=[
                pltpu.VMEM((pairs, rows, PAIR), BF16),
                pltpu.VMEM((rows, width), BF16),
                pltpu.VMEM((width, width), BF16),
                pltpu.VMEM((width, width), BF16),
                pltpu.SemaphoreType.DMA((3,)),
            ],
        ),
        compiler_params=params(WIDE),
        cost_estimate=cost(16 * rows * count * width, 28 * rows * width, 12 * rows * count),
    )(live, projected, anchor_kv, anchor_kv, *state, block_attn, w_out, w_cross_out)


def after(*arrays):
    return lax.optimization_barrier(arrays)


def permute(array, target):
    size = lax.axis_size("dom")
    pairs = [(i, target(i)) for i in range(size) if 0 <= target(i) < size]
    return lax.ppermute(array, "dom", pairs)


def local(
    points,
    norm_gain,
    w_qkv,
    w_out,
    w_cross_q,
    w_cross_kv,
    w_cross_out,
    live_blocks,
    send_blocks,
    neighbours,
    neighbour_count,
    anchor_index,
):
    rows, width = points.shape
    size = lax.axis_size("dom")
    column, ring = 2, 4
    anchors, to_prev, to_next = pick(points, norm_gain, send_blocks, anchor_index)

    def around(array):
        return [permute(array, lambda i, n=n: (i + n * ring) % size) for n in (1, -1, 2)]

    beside = permute(anchors, lambda i: i ^ column)
    low = permute(to_next, lambda i: i + 1)
    high = permute(to_prev, lambda i: i - 1)
    rows_here = around(anchors)
    points, anchors = after(points, anchors)
    projected = project(points, norm_gain, w_qkv, w_cross_q)
    beside, rows_here[0], rows_here[1], projected = after(
        beside, rows_here[0], rows_here[1], projected
    )
    rows_beside = [permute(rows_here[n], lambda i: i ^ column) for n in range(2)]
    rows_beside.append(permute(beside, lambda i: (i + 2 * ring) % size))
    block_attn = block_attention(
        projected, low, high, w_qkv, neighbours, neighbour_count, live_blocks
    )
    *parts, block_attn = after(anchors, beside, *rows_here, *rows_beside, block_attn)
    kv_own = anchor_project(parts, w_cross_kv)
    kv_other = permute(kv_own, lambda i: i ^ 1)
    state = cross_part(projected, kv_own)
    return finish(projected, kv_other, state, block_attn, w_out, w_cross_out, live_blocks)


def solution(mesh):
    sharded = P(("car", "dom"))
    in_specs = (
        P(("car", "dom"), None),
        P(),
        P(),
        P(),
        P(),
        P(),
        P(),
        sharded,
        sharded,
        P(("car", "dom"), None),
        sharded,
        sharded,
    )
    out_specs = P(("car", "dom"), None)
    return jax.shard_map(local, mesh=mesh, in_specs=in_specs, out_specs=out_specs, check_vma=False)
```

```python
import functools

import jax
import jax.numpy as jnp
from jax import lax
from jax.experimental import pallas as pl
from jax.experimental.pallas import tpu as pltpu
from jax.sharding import PartitionSpec as P

HEADS = 12
BLK = 128
HB = 2
PAIR = 128
HALF = 64
CHUNK = 512
SCALE = HALF**-0.5 * 1.4426950408889634
LIMIT = 32 * 2**20
WIDE = 61 * 2**20
NEG = -1e30
F32 = jnp.float32
BF16 = jnp.bfloat16


def params(limit=LIMIT):
    return pltpu.CompilerParams(vmem_limit_bytes=limit)


def cost(flops, nbytes, trans=0):
    return pl.CostEstimate(flops=int(flops), bytes_accessed=int(nbytes), transcendentals=int(trans))


def struct(rows, cols, dtype=BF16):
    return jax.ShapeDtypeStruct((rows, cols), dtype)


def whole(array):
    return pl.BlockSpec(array.shape, lambda *_: (0,) * array.ndim)


def mm(a, b):
    return jnp.dot(a, b, preferred_element_type=F32)


def mm_t(a, b):
    return lax.dot_general(a, b, (((1,), (1,)), ((), ())), preferred_element_type=F32)


def normed_rows(rows, gain):
    floats = rows.astype(F32)
    factor = lax.rsqrt(jnp.mean(floats * floats, axis=-1, keepdims=True) + 1e-06)
    return (floats * factor * gain).astype(BF16)


def pick_kernel(
    send_ref,
    index_ref,
    gain_ref,
    source_ref,
    anchor_ref,
    prev_ref,
    next_ref,
    out_ref,
    points_ref,
    normed_ref,
    sems,
):
    rows = points_ref.shape[0]
    tile = rows // 4
    fetch = pltpu.make_async_copy(source_ref, points_ref, sems.at[0])
    store = pltpu.make_async_copy(normed_ref, out_ref, sems.at[1])
    fetch.start()
    anchors = index_ref.shape[1]
    slot = lax.broadcasted_iota(jnp.int32, (rows, anchors), 0)
    chosen = jnp.where(slot == index_ref[...], 1.0, 0.0).astype(BF16)
    fetch.wait()
    for at in range(0, rows, tile):
        normed_ref[at : at + tile, :] = normed_rows(points_ref[at : at + tile, :], gain_ref[...])
    store.start()
    anchor_ref[...] = lax.dot_general(
        chosen, normed_ref[...], (((0,), (0,)), ((), ())), preferred_element_type=F32
    ).astype(BF16)
    for place in range(HB):
        for base, side_ref in ((0, prev_ref), (HB, next_ref)):
            start = pl.multiple_of(send_ref[base + place] * BLK, BLK)
            side_ref[place * BLK : (place + 1) * BLK, :] = normed_ref[pl.ds(start, BLK), :]
    store.wait()


def pick(points, gain, send_blocks, anchor_index):
    rows, width = points.shape
    anchors = anchor_index.shape[0]
    index = anchor_index.reshape(1, anchors)
    own = struct(anchors, width)
    side = struct(HB * BLK, width)
    vmem = pl.BlockSpec(memory_space=pltpu.VMEM)
    hbm = pl.BlockSpec(memory_space=pltpu.HBM)
    return pl.pallas_call(
        pick_kernel,
        out_shape=(own, side, side, struct(rows, width)),
        in_specs=[pl.BlockSpec(memory_space=pltpu.SMEM), vmem, vmem, hbm],
        out_specs=(vmem, vmem, vmem, hbm),
        scratch_shapes=[
            pltpu.VMEM((rows, width), BF16),
            pltpu.VMEM((rows, width), BF16),
            pltpu.SemaphoreType.DMA((2,)),
        ],
        compiler_params=params(WIDE),
        cost_estimate=cost(2 * anchors * rows * width, 6 * rows * width),
    )(send_blocks, index, gain, points)


def project_kernel(normed_ref, wqkv_ref, wcq_ref, out_ref):
    width = normed_ref.shape[1]
    for at in range(0, 3 * width, width):
        made = mm(normed_ref[...], wqkv_ref[:, at : at + width])
        out_ref[:, at : at + width] = (made * SCALE if at == 0 else made).astype(BF16)
    out_ref[:, 3 * width :] = (mm(normed_ref[...], wcq_ref[...]) * SCALE).astype(BF16)


def project(normed, w_qkv, w_cross_q):
    rows, width = normed.shape
    vmem = pl.BlockSpec(memory_space=pltpu.VMEM)
    return pl.pallas_call(
        project_kernel,
        out_shape=struct(rows, 4 * width),
        in_specs=[vmem] * 3,
        out_specs=vmem,
        compiler_params=params(24 * 2**20),
        cost_estimate=cost(2 * rows * width * 4 * width, 20 * rows * width),
    )(normed, w_qkv, w_cross_q)


def split_heads(rows):
    lane = lax.broadcasted_iota(jnp.int32, rows.shape, 1)
    zero = jnp.zeros_like(rows)
    return jnp.concatenate(
        [jnp.where(lane < HALF, rows, zero), jnp.where(lane >= HALF, rows, zero)], axis=0
    )


def join_heads(both):
    count = both.shape[0] // 2
    lane = lax.broadcasted_iota(jnp.int32, (count, PAIR), 1)
    return jnp.where(lane < HALF, both[:count], both[count:])


def weigh(weights, values):
    weights = weights.astype(BF16)
    count = weights.shape[0] // 2
    lane = lax.broadcasted_iota(jnp.int32, values.shape, 1)
    one = jnp.ones_like(values)
    return jnp.concatenate(
        [
            mm(weights[:count], jnp.where(lane < HALF, values, one)),
            mm(weights[count:], jnp.where(lane < HALF, one, values)),
        ],
        axis=0,
    )


def weigh_wide(weights, values):
    ones = jnp.ones((values.shape[0], PAIR), BF16)
    return mm(weights.astype(BF16), jnp.concatenate([values, ones], axis=1))


def block_kernel(
    ids_ref,
    count_ref,
    live_ref,
    projected_ref,
    low_ref,
    high_ref,
    weight_ref,
    out_ref,
    table_ref,
):
    width = low_ref.shape[1]

    normed = jnp.concatenate([low_ref[...], high_ref[...]], axis=0)
    for n in range(2):
        table_ref[n] = mm(normed, weight_ref[:, (1 + n) * width : (2 + n) * width]).astype(BF16)

    @pl.loop(0, count_ref.shape[0])
    def _(block):
        attend_block(block, ids_ref, count_ref, live_ref, projected_ref, table_ref, out_ref)


def attend_block(block, ids_ref, count_ref, live_ref, projected_ref, table_ref, out_ref):
    slots = ids_ref.shape[1]
    blocks = count_ref.shape[0]
    width = out_ref.shape[1]
    here = pl.ds(pl.multiple_of(block * BLK, BLK), BLK)
    count = count_ref[block]
    pairs = jnp.where(block < live_ref[0], (count + 1) // 2, 0)

    @pl.when(pairs == 0)
    def _():
        out_ref[here, :] = jnp.zeros((BLK, width), BF16)

    for used in range(1, slots // 2 + 1):

        @pl.when(pairs == used)
        def _(used=used):
            places = []
            for n in range(2 * used):
                place = ids_ref[block, n]
                own = pl.multiple_of(jnp.minimum(place, blocks - 1) * BLK, BLK)
                received = pl.multiple_of(jnp.maximum(place - blocks, 0) * BLK, BLK)
                places.append((place < blocks, own, received))
            dropped = jnp.where(count == 2 * used, 0.0, NEG)

            def rows_of(which, part, at):
                lanes = slice((1 + which) * width + at, (1 + which) * width + at + PAIR)
                return jnp.concatenate(
                    [
                        jnp.where(
                            is_own,
                            projected_ref[pl.ds(own, BLK), lanes],
                            table_ref[which, pl.ds(received, BLK), at : at + PAIR],
                        )
                        for is_own, own, received in places[2 * part : 2 * part + 2]
                    ],
                    axis=0,
                )

            for at in range(0, width, PAIR):
                query = split_heads(projected_ref[here, at : at + PAIR])
                scores = [mm_t(query, rows_of(0, part, at)) for part in range(used)]
                last = scores[-1]
                scores[-1] = jnp.concatenate([last[:, :BLK], last[:, BLK:] + dropped], axis=1)
                top = functools.reduce(jnp.maximum, scores)
                top = jnp.max(top, axis=1, keepdims=True)
                total = sum(
                    weigh_wide(jnp.exp2(scores[part] - top), rows_of(1, part, at))
                    for part in range(used)
                )
                out_ref[here, at : at + PAIR] = join_heads(
                    total[:, :PAIR] / total[:, PAIR:]
                ).astype(BF16)


def block_attention(projected, low, high, w_qkv, ids, counts, live):
    rows = projected.shape[0]
    width = low.shape[1]
    side = low.shape[0]
    vmem = pl.BlockSpec(memory_space=pltpu.VMEM)
    smem = pl.BlockSpec(memory_space=pltpu.SMEM)
    return pl.pallas_call(
        block_kernel,
        out_shape=struct(rows, width),
        in_specs=[smem] * 3 + [vmem] * 4,
        out_specs=vmem,
        scratch_shapes=[pltpu.VMEM((2, 2 * side, width), BF16)],
        compiler_params=params(),
        cost_estimate=cost(16 * rows * 5 * BLK * width, 12 * rows * width, rows * 5 * BLK * 12),
    )(ids, counts, live, projected, low, high, w_qkv)


def anchor_kernel(count, *refs):
    parts = refs[:count]
    weight_ref, out_ref, held_ref, sems = refs[count:]
    rows, width = parts[0].shape
    group = count // 2
    stores = []
    for first in range(0, count, group):
        normed = jnp.concatenate([part[...] for part in parts[first : first + group]], axis=0)
        for n in range(2):
            columns = slice(n * width, (n + 1) * width)
            slot = len(stores)
            held_ref[slot] = mm(normed, weight_ref[:, columns]).astype(BF16)
            store = pltpu.make_async_copy(
                held_ref.at[slot],
                out_ref.at[first * rows : (first + group) * rows, columns],
                sems.at[slot],
            )
            store.start()
            stores.append(store)
    for store in stores:
        store.wait()


def anchor_project(parts, weight):
    rows, width = parts[0].shape
    every = len(parts) * rows
    vmem = pl.BlockSpec(memory_space=pltpu.VMEM)
    return pl.pallas_call(
        functools.partial(anchor_kernel, len(parts)),
        out_shape=struct(every, 2 * width),
        in_specs=[vmem] * (len(parts) + 1),
        out_specs=pl.BlockSpec(memory_space=pltpu.HBM),
        scratch_shapes=[
            pltpu.VMEM((4, every // 2, width), BF16),
            pltpu.SemaphoreType.DMA((4,)),
        ],
        compiler_params=params(),
        cost_estimate=cost(4 * every * width * width, 6 * every * width),
    )(*parts, weight)


def sweep(query, keys_ref, values_ref):
    top, total = None, None
    for start in range(0, keys_ref.shape[0], CHUNK):
        scores = mm_t(query, keys_ref[start : start + CHUNK, :])
        values = values_ref[start : start + CHUNK, :]
        here = jnp.max(scores, axis=1, keepdims=True)
        if top is None:
            top = here
            total = weigh(jnp.exp2(scores - top), values)
        else:
            later = jnp.maximum(top, here)
            total = total * jnp.exp2(top - later) + weigh(jnp.exp2(scores - later), values)
            top = later
    sums = pltpu.roll(total, HALF, 1)
    return join_heads(total / sums), join_heads(top + jnp.log2(sums))


def cross_kernel(queries_ref, keys_ref, values_ref, mean_ref, size_ref):
    query = split_heads(queries_ref[...])
    mean_ref[...], size_ref[...] = sweep(query, keys_ref, values_ref)


def cross_part(projected, anchor_kv):
    rows = projected.shape[0]
    width = projected.shape[1] // 4
    count = anchor_kv.shape[0]
    pairs = width // PAIR
    tile = rows
    state = struct(rows, width, F32)
    spec = pl.BlockSpec((tile, PAIR), lambda h, i: (i, h))
    return pl.pallas_call(
        cross_kernel,
        out_shape=(state, state),
        grid=(pairs, rows // tile),
        in_specs=[
            pl.BlockSpec((tile, PAIR), lambda h, i: (i, 3 * pairs + h)),
            pl.BlockSpec((count, PAIR), lambda h, i: (0, h)),
            pl.BlockSpec((count, PAIR), lambda h, i: (0, pairs + h)),
        ],
        out_specs=[spec, spec],
        compiler_params=params(WIDE),
        cost_estimate=cost(16 * rows * count * width, 20 * rows * width, 12 * rows * count),
    )(projected, anchor_kv, anchor_kv)


def final_kernel(
    live_ref,
    queries_ref,
    keys_ref,
    values_ref,
    mean_ref,
    size_ref,
    block_source_ref,
    wout_source_ref,
    wcross_source_ref,
    out_ref,
    held_ref,
    block_ref,
    wout_ref,
    wcross_ref,
    sems,
):
    pair = pl.program_id(0)
    rows = queries_ref.shape[0]
    fetches = [
        pltpu.make_async_copy(source, target, sems.at[n])
        for n, (source, target) in enumerate(
            [
                (block_source_ref, block_ref),
                (wout_source_ref, wout_ref),
                (wcross_source_ref, wcross_ref),
            ]
        )
    ]

    @pl.when(pair == 0)
    def _():
        for fetch in fetches:
            fetch.start()

    query = split_heads(queries_ref[...])
    mean, size = sweep(query, keys_ref, values_ref)
    top = jnp.maximum(size, size_ref[...])
    share, other = jnp.exp2(size - top), jnp.exp2(size_ref[...] - top)
    held_ref[pair] = ((mean * share + mean_ref[...] * other) / (share + other)).astype(BF16)

    @pl.when(pair == pl.num_programs(0) - 1)
    def _():
        for fetch in fetches:
            fetch.wait()
        cross = jnp.concatenate([held_ref[n] for n in range(held_ref.shape[0])], axis=1)
        mixed = mm(block_ref[...], wout_ref[...]) + mm(cross, wcross_ref[...])
        place = lax.broadcasted_iota(jnp.int32, (rows, 1), 0)
        out_ref[...] = jnp.where(place // BLK < live_ref[0], mixed, 0.0).astype(BF16)


def finish(projected, anchor_kv, state, block_attn, w_out, w_cross_out, live):
    rows = projected.shape[0]
    width = projected.shape[1] // 4
    count = anchor_kv.shape[0]
    pairs = width // PAIR
    spec = pl.BlockSpec((rows, PAIR), lambda h, *_: (0, h))
    hbm = pl.BlockSpec(memory_space=pltpu.HBM)
    return pl.pallas_call(
        final_kernel,
        out_shape=struct(rows, width),
        grid_spec=pltpu.PrefetchScalarGridSpec(
            num_scalar_prefetch=1,
            grid=(pairs,),
            in_specs=[
                pl.BlockSpec((rows, PAIR), lambda h, *_: (0, 3 * pairs + h)),
                pl.BlockSpec((count, PAIR), lambda h, *_: (0, h)),
                pl.BlockSpec((count, PAIR), lambda h, *_: (0, pairs + h)),
                spec,
                spec,
                hbm,
                hbm,
                hbm,
            ],
            out_specs=pl.BlockSpec((rows, width), lambda h, *_: (0, 0)),
            scratch_shapes=[
                pltpu.VMEM((pairs, rows, PAIR), BF16),
                pltpu.VMEM((rows, width), BF16),
                pltpu.VMEM((width, width), BF16),
                pltpu.VMEM((width, width), BF16),
                pltpu.SemaphoreType.DMA((3,)),
            ],
        ),
        compiler_params=params(WIDE),
        cost_estimate=cost(16 * rows * count * width, 28 * rows * width, 12 * rows * count),
    )(live, projected, anchor_kv, anchor_kv, *state, block_attn, w_out, w_cross_out)


def after(*arrays):
    return lax.optimization_barrier(arrays)


def permute(array, target):
    size = lax.axis_size("dom")
    pairs = [(i, target(i)) for i in range(size) if 0 <= target(i) < size]
    return lax.ppermute(array, "dom", pairs)


def local(
    points,
    norm_gain,
    w_qkv,
    w_out,
    w_cross_q,
    w_cross_kv,
    w_cross_out,
    live_blocks,
    send_blocks,
    neighbours,
    neighbour_count,
    anchor_index,
):
    size = lax.axis_size("dom")
    column, ring = 2, 4
    anchors, to_prev, to_next, normed = pick(points, norm_gain, send_blocks, anchor_index)

    def around(array):
        return [permute(array, lambda i, n=n: (i + n * ring) % size) for n in (1, -1, 2)]

    beside = permute(anchors, lambda i: i ^ column)
    low = permute(to_next, lambda i: i + 1)
    high = permute(to_prev, lambda i: i - 1)
    rows_here = around(anchors)
    projected = project(normed, w_qkv, w_cross_q)
    beside, rows_here[0], rows_here[1], projected = after(
        beside, rows_here[0], rows_here[1], projected
    )
    rows_beside = [permute(rows_here[n], lambda i: i ^ column) for n in range(2)]
    rows_beside.append(permute(beside, lambda i: (i + 2 * ring) % size))
    block_attn = block_attention(
        projected, low, high, w_qkv, neighbours, neighbour_count, live_blocks
    )
    *parts, block_attn = after(anchors, beside, *rows_here, *rows_beside, block_attn)
    kv_own = anchor_project(parts, w_cross_kv)
    kv_other = permute(kv_own, lambda i: i ^ 1)
    state = cross_part(projected, kv_own)
    return finish(projected, kv_other, state, block_attn, w_out, w_cross_out, live_blocks)


def solution(mesh):
    sharded = P(("car", "dom"))
    in_specs = (
        P(("car", "dom"), None),
        P(),
        P(),
        P(),
        P(),
        P(),
        P(),
        sharded,
        sharded,
        P(("car", "dom"), None),
        sharded,
        sharded,
    )
    out_specs = P(("car", "dom"), None)
    return jax.shard_map(local, mesh=mesh, in_specs=in_specs, out_specs=out_specs, check_vma=False)
```

```python
import functools

import jax
import jax.numpy as jnp
from jax import lax
from jax.experimental import pallas as pl
from jax.experimental.pallas import tpu as pltpu
from jax.sharding import PartitionSpec as P

HEADS = 12
BLK = 128
HB = 2
PAIR = 128
HALF = 64
CHUNK = 512
SCALE = HALF**-0.5 * 1.4426950408889634
LIMIT = 32 * 2**20
WIDE = 61 * 2**20
NEG = -1e30
F32 = jnp.float32
BF16 = jnp.bfloat16


def params(limit=LIMIT):
    return pltpu.CompilerParams(vmem_limit_bytes=limit)


def cost(flops, nbytes, trans=0):
    return pl.CostEstimate(flops=int(flops), bytes_accessed=int(nbytes), transcendentals=int(trans))


def struct(rows, cols, dtype=BF16):
    return jax.ShapeDtypeStruct((rows, cols), dtype)


def whole(array):
    return pl.BlockSpec(array.shape, lambda *_: (0,) * array.ndim)


def mm(a, b):
    return jnp.dot(a, b, preferred_element_type=F32)


def mm_t(a, b):
    return lax.dot_general(a, b, (((1,), (1,)), ((), ())), preferred_element_type=F32)


def normed_rows(rows, gain):
    floats = rows.astype(F32)
    factor = lax.rsqrt(jnp.mean(floats * floats, axis=-1, keepdims=True) + 1e-06)
    return (floats * factor * gain).astype(BF16)


def pick_kernel(
    send_ref, index_ref, gain_ref, source_ref, anchor_ref, prev_ref, next_ref, points_ref, sem
):
    copy = pltpu.make_async_copy(source_ref, points_ref, sem)
    copy.start()
    rows = points_ref.shape[0]
    anchors = index_ref.shape[1]
    slot = lax.broadcasted_iota(jnp.int32, (rows, anchors), 0)
    chosen = jnp.where(slot == index_ref[...], 1.0, 0.0).astype(BF16)
    copy.wait()
    picked = lax.dot_general(
        chosen, points_ref[...], (((0,), (0,)), ((), ())), preferred_element_type=F32
    )
    anchor_ref[...] = normed_rows(picked, gain_ref[...])
    for place in range(HB):
        for base, out_ref in ((0, prev_ref), (HB, next_ref)):
            start = pl.multiple_of(send_ref[base + place] * BLK, BLK)
            out_ref[place * BLK : (place + 1) * BLK, :] = normed_rows(
                points_ref[pl.ds(start, BLK), :], gain_ref[...]
            )


def pick(points, gain, send_blocks, anchor_index):
    rows, width = points.shape
    anchors = anchor_index.shape[0]
    index = anchor_index.reshape(1, anchors)
    own = struct(anchors, width)
    side = struct(HB * BLK, width)
    vmem = pl.BlockSpec(memory_space=pltpu.VMEM)
    return pl.pallas_call(
        pick_kernel,
        out_shape=(own, side, side),
        in_specs=[
            pl.BlockSpec(memory_space=pltpu.SMEM),
            vmem,
            vmem,
            pl.BlockSpec(memory_space=pltpu.HBM),
        ],
        scratch_shapes=[pltpu.VMEM((rows, width), BF16), pltpu.SemaphoreType.DMA],
        compiler_params=params(WIDE),
        cost_estimate=cost(2 * anchors * rows * width, 4 * rows * width),
    )(send_blocks, index, gain, points)


def project_kernel(points_ref, gain_ref, wqkv_ref, wcq_ref, out_ref, normed_ref):
    rows, width = points_ref.shape
    tile = rows // 4
    for at in range(0, rows, tile):
        normed = normed_rows(points_ref[at : at + tile, :], gain_ref[...])
        normed_ref[at : at + tile, :] = normed
        out_ref[at : at + tile, :width] = (mm(normed, wqkv_ref[:, :width]) * SCALE).astype(BF16)
    for at in range(width, 3 * width, width):
        out_ref[:, at : at + width] = mm(normed_ref[...], wqkv_ref[:, at : at + width]).astype(BF16)
    out_ref[:, 3 * width :] = (mm(normed_ref[...], wcq_ref[...]) * SCALE).astype(BF16)


def project(points, gain, w_qkv, w_cross_q):
    rows, width = points.shape
    vmem = pl.BlockSpec(memory_space=pltpu.VMEM)
    return pl.pallas_call(
        project_kernel,
        out_shape=struct(rows, 4 * width),
        in_specs=[vmem] * 4,
        out_specs=vmem,
        scratch_shapes=[pltpu.VMEM((rows, width), BF16)],
        compiler_params=params(24 * 2**20),
        cost_estimate=cost(2 * rows * width * 4 * width, 20 * rows * width),
    )(points, gain, w_qkv, w_cross_q)


def split_heads(rows):
    lane = lax.broadcasted_iota(jnp.int32, rows.shape, 1)
    zero = jnp.zeros_like(rows)
    return jnp.concatenate(
        [jnp.where(lane < HALF, rows, zero), jnp.where(lane >= HALF, rows, zero)], axis=0
    )


def join_heads(both):
    count = both.shape[0] // 2
    lane = lax.broadcasted_iota(jnp.int32, (count, PAIR), 1)
    return jnp.where(lane < HALF, both[:count], both[count:])


def weigh(weights, values):
    weights = weights.astype(BF16)
    count = weights.shape[0] // 2
    lane = lax.broadcasted_iota(jnp.int32, values.shape, 1)
    one = jnp.ones_like(values)
    return jnp.concatenate(
        [
            mm(weights[:count], jnp.where(lane < HALF, values, one)),
            mm(weights[count:], jnp.where(lane < HALF, one, values)),
        ],
        axis=0,
    )


def weigh_wide(weights, values):
    ones = jnp.ones((values.shape[0], PAIR), BF16)
    return mm(weights.astype(BF16), jnp.concatenate([values, ones], axis=1))


def block_kernel(
    ids_ref,
    count_ref,
    live_ref,
    projected_ref,
    low_ref,
    high_ref,
    weight_ref,
    out_ref,
    table_ref,
    sems,
):
    rows = projected_ref.shape[0]
    width = low_ref.shape[1]

    copies = [
        pltpu.make_async_copy(
            projected_ref.at[:, (1 + n) * width : (2 + n) * width],
            table_ref.at[n, :rows],
            sems.at[n],
        )
        for n in range(2)
    ]
    for copy in copies:
        copy.start()
    normed = jnp.concatenate([low_ref[...], high_ref[...]], axis=0)
    for n in range(2):
        made = mm(normed, weight_ref[:, (1 + n) * width : (2 + n) * width])
        table_ref[n, rows:, :] = made.astype(BF16)
    for copy in copies:
        copy.wait()

    @pl.loop(0, count_ref.shape[0])
    def _(block):
        attend_block(block, ids_ref, count_ref, live_ref, projected_ref, table_ref, out_ref)


def attend_block(block, ids_ref, count_ref, live_ref, projected_ref, table_ref, out_ref):
    slots = ids_ref.shape[1]
    width = out_ref.shape[1]
    here = pl.ds(pl.multiple_of(block * BLK, BLK), BLK)
    count = count_ref[block]
    pairs = jnp.where(block < live_ref[0], (count + 1) // 2, 0)

    @pl.when(pairs == 0)
    def _():
        out_ref[here, :] = jnp.zeros((BLK, width), BF16)

    for used in range(1, slots // 2 + 1):

        @pl.when(pairs == used)
        def _(used=used):
            starts = [pl.multiple_of(ids_ref[block, n] * BLK, BLK) for n in range(2 * used)]
            dropped = jnp.where(count == 2 * used, 0.0, NEG)

            def rows_of(which, part, at):
                return jnp.concatenate(
                    [
                        table_ref[which, pl.ds(start, BLK), at : at + PAIR]
                        for start in starts[2 * part : 2 * part + 2]
                    ],
                    axis=0,
                )

            for at in range(0, width, PAIR):
                query = split_heads(projected_ref[here, at : at + PAIR])
                scores = [mm_t(query, rows_of(0, part, at)) for part in range(used)]
                last = scores[-1]
                scores[-1] = jnp.concatenate([last[:, :BLK], last[:, BLK:] + dropped], axis=1)
                top = functools.reduce(jnp.maximum, scores)
                top = jnp.max(top, axis=1, keepdims=True)
                total = sum(
                    weigh_wide(jnp.exp2(scores[part] - top), rows_of(1, part, at))
                    for part in range(used)
                )
                out_ref[here, at : at + PAIR] = join_heads(
                    total[:, :PAIR] / total[:, PAIR:]
                ).astype(BF16)


def block_attention(projected, low, high, w_qkv, ids, counts, live):
    rows = projected.shape[0]
    width = low.shape[1]
    side = low.shape[0]
    vmem = pl.BlockSpec(memory_space=pltpu.VMEM)
    smem = pl.BlockSpec(memory_space=pltpu.SMEM)
    return pl.pallas_call(
        block_kernel,
        out_shape=struct(rows, width),
        in_specs=[smem] * 3 + [vmem] * 4,
        out_specs=vmem,
        scratch_shapes=[
            pltpu.VMEM((2, rows + 2 * side, width), BF16),
            pltpu.SemaphoreType.DMA((2,)),
        ],
        compiler_params=params(),
        cost_estimate=cost(16 * rows * 5 * BLK * width, 12 * rows * width, rows * 5 * BLK * 12),
    )(ids, counts, live, projected, low, high, w_qkv)


def anchor_kernel(count, *refs):
    parts = refs[:count]
    weight_ref, out_ref, held_ref, sems = refs[count:]
    rows, width = parts[0].shape
    group = count // 2
    stores = []
    for first in range(0, count, group):
        normed = jnp.concatenate([part[...] for part in parts[first : first + group]], axis=0)
        for n in range(2):
            columns = slice(n * width, (n + 1) * width)
            slot = len(stores)
            held_ref[slot] = mm(normed, weight_ref[:, columns]).astype(BF16)
            store = pltpu.make_async_copy(
                held_ref.at[slot],
                out_ref.at[first * rows : (first + group) * rows, columns],
                sems.at[slot],
            )
            store.start()
            stores.append(store)
    for store in stores:
        store.wait()


def anchor_project(parts, weight):
    rows, width = parts[0].shape
    every = len(parts) * rows
    vmem = pl.BlockSpec(memory_space=pltpu.VMEM)
    return pl.pallas_call(
        functools.partial(anchor_kernel, len(parts)),
        out_shape=struct(every, 2 * width),
        in_specs=[vmem] * (len(parts) + 1),
        out_specs=pl.BlockSpec(memory_space=pltpu.HBM),
        scratch_shapes=[
            pltpu.VMEM((4, every // 2, width), BF16),
            pltpu.SemaphoreType.DMA((4,)),
        ],
        compiler_params=params(),
        cost_estimate=cost(4 * every * width * width, 6 * every * width),
    )(*parts, weight)


def sweep(query, keys_ref, values_ref):
    top, total = None, None
    for start in range(0, keys_ref.shape[0], CHUNK):
        scores = mm_t(query, keys_ref[start : start + CHUNK, :])
        values = values_ref[start : start + CHUNK, :]
        here = jnp.max(scores, axis=1, keepdims=True)
        if top is None:
            top = here
            total = weigh(jnp.exp2(scores - top), values)
        else:
            later = jnp.maximum(top, here)
            total = total * jnp.exp2(top - later) + weigh(jnp.exp2(scores - later), values)
            top = later
    sums = pltpu.roll(total, HALF, 1)
    return join_heads(total / sums), join_heads(top + jnp.log2(sums))


def cross_kernel(queries_ref, keys_ref, values_ref, mean_ref, size_ref):
    query = split_heads(queries_ref[...])
    mean_ref[...], size_ref[...] = sweep(query, keys_ref, values_ref)


def cross_part(projected, anchor_kv):
    rows = projected.shape[0]
    width = projected.shape[1] // 4
    count = anchor_kv.shape[0]
    pairs = width // PAIR
    tile = rows
    state = struct(rows, width, F32)
    spec = pl.BlockSpec((tile, PAIR), lambda h, i: (i, h))
    return pl.pallas_call(
        cross_kernel,
        out_shape=(state, state),
        grid=(pairs, rows // tile),
        in_specs=[
            pl.BlockSpec((tile, PAIR), lambda h, i: (i, 3 * pairs + h)),
            pl.BlockSpec((count, PAIR), lambda h, i: (0, h)),
            pl.BlockSpec((count, PAIR), lambda h, i: (0, pairs + h)),
        ],
        out_specs=[spec, spec],
        compiler_params=params(WIDE),
        cost_estimate=cost(16 * rows * count * width, 20 * rows * width, 12 * rows * count),
    )(projected, anchor_kv, anchor_kv)


def final_kernel(
    live_ref,
    queries_ref,
    keys_ref,
    values_ref,
    mean_ref,
    size_ref,
    block_source_ref,
    wout_source_ref,
    wcross_source_ref,
    out_ref,
    held_ref,
    block_ref,
    wout_ref,
    wcross_ref,
    sems,
):
    pair = pl.program_id(0)
    rows = queries_ref.shape[0]
    fetches = [
        pltpu.make_async_copy(source, target, sems.at[n])
        for n, (source, target) in enumerate(
            [
                (block_source_ref, block_ref),
                (wout_source_ref, wout_ref),
                (wcross_source_ref, wcross_ref),
            ]
        )
    ]

    @pl.when(pair == 0)
    def _():
        for fetch in fetches:
            fetch.start()

    query = split_heads(queries_ref[...])
    mean, size = sweep(query, keys_ref, values_ref)
    top = jnp.maximum(size, size_ref[...])
    share, other = jnp.exp2(size - top), jnp.exp2(size_ref[...] - top)
    held_ref[pair] = ((mean * share + mean_ref[...] * other) / (share + other)).astype(BF16)

    @pl.when(pair == pl.num_programs(0) - 1)
    def _():
        for fetch in fetches:
            fetch.wait()
        cross = jnp.concatenate([held_ref[n] for n in range(held_ref.shape[0])], axis=1)
        mixed = mm(block_ref[...], wout_ref[...]) + mm(cross, wcross_ref[...])
        place = lax.broadcasted_iota(jnp.int32, (rows, 1), 0)
        out_ref[...] = jnp.where(place // BLK < live_ref[0], mixed, 0.0).astype(BF16)


def finish(projected, anchor_kv, state, block_attn, w_out, w_cross_out, live):
    rows = projected.shape[0]
    width = projected.shape[1] // 4
    count = anchor_kv.shape[0]
    pairs = width // PAIR
    spec = pl.BlockSpec((rows, PAIR), lambda h, *_: (0, h))
    hbm = pl.BlockSpec(memory_space=pltpu.HBM)
    return pl.pallas_call(
        final_kernel,
        out_shape=struct(rows, width),
        grid_spec=pltpu.PrefetchScalarGridSpec(
            num_scalar_prefetch=1,
            grid=(pairs,),
            in_specs=[
                pl.BlockSpec((rows, PAIR), lambda h, *_: (0, 3 * pairs + h)),
                pl.BlockSpec((count, PAIR), lambda h, *_: (0, h)),
                pl.BlockSpec((count, PAIR), lambda h, *_: (0, pairs + h)),
                spec,
                spec,
                hbm,
                hbm,
                hbm,
            ],
            out_specs=pl.BlockSpec((rows, width), lambda h, *_: (0, 0)),
            scratch_shapes=[
                pltpu.VMEM((pairs, rows, PAIR), BF16),
                pltpu.VMEM((rows, width), BF16),
                pltpu.VMEM((width, width), BF16),
                pltpu.VMEM((width, width), BF16),
                pltpu.SemaphoreType.DMA((3,)),
            ],
        ),
        compiler_params=params(WIDE),
        cost_estimate=cost(16 * rows * count * width, 28 * rows * width, 12 * rows * count),
    )(live, projected, anchor_kv, anchor_kv, *state, block_attn, w_out, w_cross_out)


def after(*arrays):
    return lax.optimization_barrier(arrays)


def permute(array, target):
    size = lax.axis_size("dom")
    pairs = [(i, target(i)) for i in range(size) if 0 <= target(i) < size]
    return lax.ppermute(array, "dom", pairs)


def local(
    points,
    norm_gain,
    w_qkv,
    w_out,
    w_cross_q,
    w_cross_kv,
    w_cross_out,
    live_blocks,
    send_blocks,
    neighbours,
    neighbour_count,
    anchor_index,
):
    rows, width = points.shape
    size = lax.axis_size("dom")
    column, ring = 2, 4
    anchors, to_prev, to_next = pick(points, norm_gain, send_blocks, anchor_index)

    def around(array):
        return [permute(array, lambda i, n=n: (i + n * ring) % size) for n in (1, -1, 2)]

    beside = permute(anchors, lambda i: i ^ column)
    low = permute(to_next, lambda i: i + 1)
    high = permute(to_prev, lambda i: i - 1)
    rows_here = around(anchors)
    points, anchors = after(points, anchors)
    projected = project(points, norm_gain, w_qkv, w_cross_q)
    beside, rows_here[0], rows_here[1], projected = after(
        beside, rows_here[0], rows_here[1], projected
    )
    rows_beside = [permute(rows_here[n], lambda i: i ^ column) for n in range(2)]
    rows_beside.append(permute(beside, lambda i: (i + 2 * ring) % size))
    block_attn = block_attention(
        projected, low, high, w_qkv, neighbours, neighbour_count, live_blocks
    )
    *parts, block_attn = after(anchors, beside, *rows_here, *rows_beside, block_attn)
    kv_own = anchor_project(parts, w_cross_kv)
    kv_other = permute(kv_own, lambda i: i ^ 1)
    state = cross_part(projected, kv_own)
    return finish(projected, kv_other, state, block_attn, w_out, w_cross_out, live_blocks)


def solution(mesh):
    sharded = P(("car", "dom"))
    in_specs = (
        P(("car", "dom"), None),
        P(),
        P(),
        P(),
        P(),
        P(),
        P(),
        sharded,
        sharded,
        P(("car", "dom"), None),
        sharded,
        sharded,
    )
    out_specs = P(("car", "dom"), None)
    return jax.shard_map(local, mesh=mesh, in_specs=in_specs, out_specs=out_specs, check_vma=False)
```
